32 devices in a mesh: tile: 8 (over y, x, core), rep: 4 (over z).
Axes of the slice: x: 2, y: 2, z: 4, core: 2. Of those that a mesh axis runs over, the one named last changes fastest.
Arguments:
- features: bfloat16 [4, 32, 64, 512], P('rep', None, 'tile'), may hold values from -6 to 6
- cotangent: bfloat16 [4, 32, 64, 512], P('rep', None, 'tile'), may hold values from -6 to 6
- positions: int32 [4, 64], P('rep', 'tile'), may hold values from 0 to 16, as said below
- weight_first: bfloat16 [27, 32, 32], replicated, may hold values from -0.21875 to 0.21875
- weight_second: bfloat16 [27, 32, 32], replicated, may hold values from -0.21875 to 0.21875
- gain_first: float32 [32], replicated, may hold values from 0.4 to 1.6
- bias_first: float32 [32], replicated, may hold values from -3 to 3
- gain_second: float32 [32], replicated, may hold values from 0.4 to 1.6
- bias_second: float32 [32], replicated, may hold values from -3 to 3
Outputs:
- block_output: bfloat16 [4, 32, 64, 512], P('rep', None, 'tile')
- block_grad: bfloat16 [4, 32, 64, 512], P('rep', None, 'tile')
- grad_first: float32 [27, 32, 32], replicated
- grad_second: float32 [27, 32, 32], replicated
The draws below stay inside these ranges and needn't reach their ends.
Inputs may be any that keep to these rules, and one draw needn't show every extreme that they name: In each region, a tile's 8 entries hold the positions of its active blocks in increasing order, then 16 in the entries left; every tile has at least one active block and some tile of every region has 8.
All inputs are finite; a program needn't handle non-finite values.
Results may differ from the reference program's by a relative error of at most 0.0057.
Values may be sent and summed in bfloat16 or wider, within the bound.
A program may use at most 128 MiB of HBM per device.

```python
import jax
import jax.numpy as jnp
from jax import lax

C = 32
BS = 8
PX = 4
PY = 2
PZ = 2
TGY = 4
NPOS = 16
NB = 8
TILES = 8
REGIONS = 4
VOXELS = 131072
N_TILE = 8
N_REP = 4


def draw_positions(key, part):
    key = jax.random.fold_in(key, 11)
    key_count, key_pick, key_full = jax.random.split(key, 3)
    rolls = jax.random.randint(key_count, (N_REP, N_TILE), 0, 17)
    counts = 1 + rolls * rolls * (NB - 1) // 256
    full_tile = jax.random.randint(key_full, (N_REP, 1), 0, N_TILE)
    counts = jnp.where(jnp.arange(N_TILE)[None, :] == full_tile, NB, counts)
    scores = jax.random.randint(key_pick, (N_REP, N_TILE, NPOS), 0, 1 << 20) * NPOS + jnp.arange(NPOS)[None, None, :]
    order = jnp.argsort(scores, axis=-1)
    ranks = jnp.argsort(order, axis=-1)
    chosen = jnp.where(ranks < counts[:, :, None], jnp.arange(NPOS)[None, None, :], NPOS)
    picked = jnp.sort(chosen, axis=-1)[:, :, :NB]
    return picked.reshape(N_REP, N_TILE * NB).astype(jnp.int32)


def level_of(stream_key, shape, shards, least, high):
    gain, own = 1.0, jax.random.fold_in(stream_key, 6)
    for dim, blocks in shards:
        draws = jnp.exp(jax.random.uniform(jax.random.fold_in(own, dim), (blocks,), jnp.float32, least / len(shards), high / len(shards)))
        gain = gain * jnp.repeat(draws, shape[dim] // blocks).reshape([-1 if axis == dim else 1 for axis in range(len(shape))])
    return gain


def centred(stream_key, dims, scale, most, shards=(), kind=jnp.bfloat16):
    array = scale * jax.random.normal(stream_key, dims, jnp.float32)
    if shards:
        array = array * level_of(stream_key, dims, shards, -0.22, 0.18)
    return jnp.clip(array, -most, most).astype(kind)


def setup_inputs(seed: int = 0) -> dict:
    seeds = jax.random.split(jax.random.key(seed), 10)
    return {
        "features": centred(seeds[0], (REGIONS, C, TILES * NB, BS ** 3), 1.0, 6.0, ((0, 4), (2, 8))),
        "cotangent": centred(seeds[1], (REGIONS, C, TILES * NB, BS ** 3), 1.0, 6.0, ((0, 4), (2, 8))),
        "positions": draw_positions(jax.random.fold_in(seeds[9], 71), 0),
        "weight_first": centred(seeds[3], (27, C, C), (27 * C) ** -0.5, 0.21875),
        "weight_second": centred(seeds[4], (27, C, C), (27 * C) ** -0.5, 0.21875),
        "gain_first": jnp.clip(1.0 + 0.12 * jax.random.normal(seeds[5], (C,), jnp.float32), 0.4, 1.6),
        "bias_first": centred(seeds[6], (C,), 0.5, 3.0, (), jnp.float32),
        "gain_second": jnp.clip(1.0 + 0.12 * jax.random.normal(seeds[7], (C,), jnp.float32), 0.4, 1.6),
        "bias_second": centred(seeds[8], (C,), 0.5, 3.0, (), jnp.float32),
    }


def tap_kernel(weights):
    return weights.reshape(3, 3, 3, C, C).transpose(3, 4, 0, 1, 2)

def convolve(field, weights):
    result = lax.conv_general_dilated(field[None], tap_kernel(weights), (1, 1, 1), [(1, 1), (1, 1), (1, 1)], dimension_numbers=('NCDHW', 'OIDHW', 'NCDHW'), precision=lax.Precision.HIGHEST)
    return result[0]

def sigmoid_slope(values):
    logistic = jax.nn.sigmoid(values)
    return logistic + values * logistic * (1.0 - logistic)

def column(vector):
    return vector[:, None, None, None]

def reference(features, cotangent, positions, weight_first, weight_second, gain_first, bias_first, gain_second, bias_second):
    volume = BS ** 3
    grid_x = N_TILE // TGY * PX
    grid_y = TGY * PY
    block_count = grid_x * grid_y * PZ
    slot_count = N_TILE * NB
    first_w = weight_first.astype(jnp.float32)
    second_w = weight_second.astype(jnp.float32)

    def region(carry, inputs):
        region_feat, region_cot, region_pos = inputs
        tile_of = jnp.arange(slot_count, dtype=jnp.int32) // NB
        valid = region_pos < NPOS
        place = jnp.where(valid, region_pos, 0)
        block_x = tile_of // TGY * PX + place // (PY * PZ)
        block_y = tile_of % TGY * PY + place // PZ % PY
        block_z = place % PZ
        target = jnp.where(valid, (block_x * grid_y + block_y) * PZ + block_z, block_count).astype(jnp.int32)

        def spread(compact):
            depth = compact.shape[0]
            blocks = jnp.zeros((depth, block_count + 1, volume), jnp.float32).at[:, target].set(compact.astype(jnp.float32))[:, :block_count]
            blocks = blocks.reshape(depth, grid_x, grid_y, PZ, BS, BS, BS).transpose(0, 1, 4, 2, 5, 3, 6)
            return blocks.reshape(depth, grid_x * BS, grid_y * BS, PZ * BS)

        def collect(grid):
            depth = grid.shape[0]
            blocks = grid.reshape(depth, grid_x, BS, grid_y, BS, PZ, BS).transpose(0, 1, 3, 5, 2, 4, 6).reshape(depth, block_count, volume)
            picked = jnp.take(blocks, jnp.minimum(target, block_count - 1), axis=1)
            return jnp.where(valid[None, :, None], picked, 0.0)
        active = spread(jnp.ones((1, slot_count, volume), jnp.float32))[0]
        field_in = spread(region_feat)
        pre_first = convolve(field_in, first_w) * column(gain_first) + column(bias_first)
        hidden = (jax.nn.silu(pre_first) * active).astype(jnp.bfloat16)
        hidden_wide = hidden.astype(jnp.float32)
        pre_second = convolve(hidden_wide, second_w) * column(gain_second) + column(bias_second) + field_in
        output = collect(jax.nn.silu(pre_second)).astype(jnp.bfloat16)
        upstream = spread(region_cot)
        d_second = upstream * sigmoid_slope(pre_second)
        e_second = (d_second * column(gain_second)).astype(jnp.bfloat16)
        unused_second, pull_second = jax.vjp(convolve, hidden_wide, second_w)
        d_hidden, grad_w_second = pull_second(e_second.astype(jnp.float32))
        d_hidden = d_hidden * active
        e_first = (d_hidden * sigmoid_slope(pre_first) * column(gain_first)).astype(jnp.bfloat16)
        unused_first, pull_first = jax.vjp(convolve, field_in, first_w)
        d_input, grad_w_first = pull_first(e_first.astype(jnp.float32))
        gradient = collect(d_second + d_input).astype(jnp.bfloat16)
        return ((carry[0] + grad_w_first, carry[1] + grad_w_second), (output, gradient))
    start = (jnp.zeros((27, C, C), jnp.float32), jnp.zeros((27, C, C), jnp.float32))
    totals, outputs = lax.scan(region, start, (features, cotangent, positions))
    scale = 1.0 / jnp.sqrt(jnp.float32(VOXELS))
    return (outputs[0], outputs[1], totals[0] * scale, totals[1] * scale)
```

```python
import functools

import jax
import jax.numpy as jnp
from jax import lax
from jax.experimental import pallas as pl
from jax.experimental.pallas import tpu as pltpu
from jax.sharding import PartitionSpec as P

BS = 8
PX = 4
PY = 2
PZ = 2
TGY = 4
C = 32
X = PX * BS
Y = PY * BS
NPOS = PX * PY * PZ
NB = 8
HALO = 2
YS = Y + 2 * HALO
ROWS = (X + 2 * HALO) * YS
BASE = 16
TOTAL = BASE + ROWS + 16
WIDE_START, WIDE_ROWS = 8, 704
OWN_START, OWN_ROWS = HALO * YS, X * YS
EMPTY = 1024.0
GROUPS = 4
LANES = 128
F32 = jnp.float32
BF16 = jnp.bfloat16
MESH = pl.DeviceIdType.MESH
SHIFTS = [(t // 3 - 1) * YS + (t % 3 - 1) for t in range(9)]
WAYS = [(-1, 0), (1, 0), (0, -1), (0, 1), (-1, -1), (-1, 1), (1, -1), (1, 1)]


def first_cell(way, extent):
    return HALO if way < 0 else extent


def landing_cell(way, extent):
    return HALO + extent if way < 0 else 0


def kernel(
    tiles_x,
    slot_of,
    slot_pos,
    feats,
    cots,
    weights,
    scales,
    out_ref,
    grad_ref,
    wgrad_ref,
    raw,
    field,
    pre_one,
    hidden,
    cot,
    d_two,
    e_two,
    e_one,
    edge,
    taps_one,
    taps_two,
    taps_back,
    corner_taps,
    band,
    band_corner,
    turned,
    staged,
    send_x,
    send_y,
    send_c,
    recv_x,
    recv_y,
    recv_c,
    send_sem,
    recv_sem,
):
    me = lax.axis_index("tile")
    tx = me // TGY
    ty = me % TGY

    def exists(way, sign):
        ix, iy = tx + sign * way[0], ty + sign * way[1]
        return (ix >= 0) & (ix < tiles_x) & (iy >= 0) & (iy < TGY)

    def partner(way, sign):
        return me + sign * (way[0] * TGY + way[1])

    recv_x[0] = jnp.full(recv_x.shape[1:], EMPTY, BF16)
    recv_y[0] = jnp.full(recv_y.shape[1:], EMPTY, BF16)
    recv_c[0] = jnp.full(recv_c.shape[1:], EMPTY, BF16)
    recv_x[1] = jnp.zeros(recv_x.shape[1:], BF16)
    recv_y[1] = jnp.zeros(recv_y.shape[1:], BF16)
    recv_c[1] = jnp.zeros(recv_c.shape[1:], BF16)

    barrier = pltpu.get_barrier_semaphore()
    for way in WAYS:
        @pl.when(exists(way, 1))
        def _():
            pl.semaphore_signal(
                barrier, inc=1, device_id={"tile": partner(way, 1)}, device_id_type=MESH
            )

    def buffers(which, number):
        if number < 2:
            return send_x.at[which, number], recv_x.at[which, number]
        if number < 4:
            return send_y.at[which, number - 2], recv_y.at[which, number - 2]
        return send_c.at[which, number - 4], recv_c.at[which, number - 4]

    def transfer(which, number, sign):
        source, target = buffers(which, number)
        return pltpu.make_async_remote_copy(
            src_ref=source,
            dst_ref=target,
            send_sem=send_sem.at[which, number],
            recv_sem=recv_sem.at[which, number],
            device_id={"tile": partner(WAYS[number], sign)},
            device_id_type=MESH,
        )

    def pack(grid, which):
        for number, (wx, wy) in enumerate(WAYS):
            for g in range(GROUPS):
                lanes = slice(g * LANES, (g + 1) * LANES)
                if number < 2:
                    for k in range(HALO):
                        row = BASE + (first_cell(wx, X) + k) * YS + HALO
                        send_x[which, number, k * Y : (k + 1) * Y, lanes] = grid[
                            g, row : row + Y, :
                        ].astype(BF16)
                elif number < 4:
                    for k in range(HALO):
                        row = BASE + OWN_START + first_cell(wy, Y) + k
                        send_y[which, number - 2, k * X : (k + 1) * X, lanes] = grid[
                            g, pl.ds(row, X, stride=YS), :
                        ].astype(BF16)
                else:
                    row = BASE + first_cell(wx, X) * YS + first_cell(wy, Y)
                    both = [grid[g, row + k * YS : row + k * YS + 8, :] for k in range(HALO)]
                    send_c[which, number - 4, :, lanes] = jnp.concatenate(both, 0).astype(BF16)

    def start(which):
        for number, way in enumerate(WAYS):
            @pl.when(exists(way, 1))
            def _():
                transfer(which, number, 1).start()

    def finish(which):
        for number, way in enumerate(WAYS):
            @pl.when(exists(way, 1))
            def _():
                transfer(which, number, 1).wait_send()

            @pl.when(exists(way, -1))
            def _():
                transfer(which, number, -1).wait_recv()

    def unpack(grid, which):
        for number, (wx, wy) in enumerate(WAYS):
            for g in range(GROUPS):
                lanes = slice(g * LANES, (g + 1) * LANES)
                if number < 2:
                    for k in range(HALO):
                        row = BASE + (landing_cell(wx, X) + k) * YS + HALO
                        grid[g, row : row + Y, :] = recv_x[
                            which, number, k * Y : (k + 1) * Y, lanes
                        ].astype(F32)
                elif number < 4:
                    for k in range(HALO):
                        row = BASE + OWN_START + landing_cell(wy, Y) + k
                        grid[g, pl.ds(row, X, stride=YS), :] = recv_y[
                            which, number - 2, k * X : (k + 1) * X, lanes
                        ].astype(F32)
                else:
                    both = recv_c[which, number - 4, :, lanes].astype(F32)
                    for k in range(HALO):
                        row = BASE + (landing_cell(wx, X) + k) * YS + landing_cell(wy, Y)
                        grid[g, row : row + HALO, :] = both[k * 8 : k * 8 + HALO]

    def block_rows(p, i):
        px, py = p // (PY * PZ), p // PZ % PY
        return BASE + (HALO + px * BS + i) * YS + HALO + py * BS

    def spread(blocks, grid):
        for p in range(NPOS):
            block = blocks[slot_of[p]].astype(F32)
            for i in range(BS):
                row = block_rows(p, i)
                for half in range(2):
                    grid[p % PZ * 2 + half, row : row + BS, :] = block[
                        i * BS : (i + 1) * BS, half * LANES : (half + 1) * LANES
                    ]

    def collect(grid, result):
        staged[NPOS] = jnp.zeros(staged.shape[1:], BF16)
        for p in range(NPOS):
            for half in range(2):
                pieces = [
                    grid[p % PZ * 2 + half, block_rows(p, i) : block_rows(p, i) + BS, :]
                    for i in range(BS)
                ]
                staged[p, :, half * LANES : (half + 1) * LANES] = jnp.concatenate(
                    pieces, 0
                ).astype(BF16)
        for s in range(NB):
            result[s] = staged[slot_pos[s]]

    for g in range(GROUPS):
        raw[g] = jnp.full((TOTAL, LANES), EMPTY, F32)
        cot[g] = jnp.zeros((TOTAL, LANES), F32)
        e_two[g] = jnp.zeros((TOTAL, LANES), F32)
    spread(feats, raw)
    pack(raw, 0)
    pl.semaphore_wait(barrier, sum(exists(way, 1).astype(jnp.int32) for way in WAYS))
    start(0)

    lane_group = lax.broadcasted_iota(jnp.int32, (C, LANES), 1) // C
    picks = [(lane_group == k).astype(F32).astype(BF16) for k in range(4)]
    for w in range(4):
        band_corner[w] = jnp.zeros(band_corner.shape[1:], BF16)

    def build(step, carry):
        w = step // 9
        t = step % 9
        three = [weights[w, t * 3 + k] for k in range(3)]
        row = pl.multiple_of(t * 256, 256)
        for z_in in range(8):
            for tile in range(2):
                total = None
                for k in range(4):
                    dz = z_in - (tile * 4 + k)
                    if abs(dz) <= 1:
                        term = three[dz + 1] * picks[k]
                        total = term if total is None else total + term
                if total is None:
                    total = jnp.zeros((C, LANES), BF16)
                band[w, pl.ds(row + z_in * C, C), tile * LANES : (tile + 1) * LANES] = total
        edge_row = pl.multiple_of(t * 64, 64)
        band_corner[w, pl.ds(edge_row, C), LANES:] = three[0] * picks[0]
        band_corner[w, pl.ds(edge_row + C, C), :LANES] = three[2] * picks[3]
        return carry

    lax.fori_loop(0, 36, build, 0)
    spread(cots, cot)

    def gather_taps(grid, taps, first, rows):
        lane = lax.broadcasted_iota(jnp.int32, (TOTAL, LANES), 1)
        pair = jnp.where(
            lane < C,
            pltpu.roll(grid[1], C, 1),
            jnp.where(lane < 2 * C, pltpu.roll(grid[2], C, 1), 0.0),
        )
        edge[0] = pair
        edge[1] = pltpu.roll(pair, 2 * C, 1)
        for t in range(9):
            begin = BASE + first + SHIFTS[t]
            for g in range(GROUPS):
                lanes = slice(t * 256 + g % 2 * LANES, t * 256 + g % 2 * LANES + LANES)
                taps[g // 2, :rows, lanes] = grid[g, begin : begin + rows, :].astype(BF16)
        for j in range(5):
            begin = BASE + first + SHIFTS[2 * j]
            value = edge[0, begin : begin + rows, :]
            if j < 4:
                begin = BASE + first + SHIFTS[2 * j + 1]
                value = value + edge[1, begin : begin + rows, :]
            corner_taps[:rows, j * LANES : (j + 1) * LANES] = value.astype(BF16)

    def convolve(taps, w, first, rows, finish_group):
        chunk = rows // 2

        def step(c, carry):
            here = pl.ds(pl.multiple_of(c * chunk, 16), chunk)
            low = jnp.dot(taps[0, here, :], band[w], preferred_element_type=F32)
            high = jnp.dot(taps[1, here, :], band[w], preferred_element_type=F32)
            mid = jnp.dot(corner_taps[here, :], band_corner[w], preferred_element_type=F32)
            there = pl.ds(pl.multiple_of(BASE + first + c * chunk, 8), chunk)
            finish_group(0, there, low[:, :LANES])
            finish_group(1, there, low[:, LANES:] + mid[:, :LANES])
            finish_group(2, there, high[:, :LANES] + mid[:, LANES:])
            finish_group(3, there, high[:, LANES:])
            return carry

        lax.fori_loop(0, 2, step, 0)

    def weight_gradient(taps, offset, which):
        for half in range(2):
            left = slice(half * 224, half * 224 + 288)

            def step(t, carry):
                lanes = pl.ds(pl.multiple_of(t * 256, 256), 256)
                product = jnp.dot(
                    turned[left, :],
                    taps[half, offset : offset + OWN_ROWS, lanes],
                    preferred_element_type=F32,
                )
                for dz in range(-1, 2):
                    total = jnp.zeros((C, LANES), F32)
                    for b in range(8):
                        a = b + half - dz
                        if 0 <= a <= 8:
                            part = product[
                                a * C : (a + 1) * C, b // 4 * LANES : (b // 4 + 1) * LANES
                            ]
                            total = total + jnp.where(lane_group == b % 4, part, 0.0)
                    total = total + pltpu.roll(total, 64, 1)
                    total = total + pltpu.roll(total, 32, 1)
                    if half == 0:
                        wgrad_ref[which, t * 3 + dz + 1] = total
                    else:
                        wgrad_ref[which, t * 3 + dz + 1] += total
                return carry

            lax.fori_loop(0, 9, step, 0)

    gain_one, bias_one = scales[0:1, :], scales[1:2, :]
    gain_two, bias_two = scales[2:3, :], scales[3:4, :]

    finish(0)
    unpack(raw, 0)
    for g in range(GROUPS):
        value = raw[g]
        field[g] = jnp.where(value < 512.0, value, 0.0)

    gather_taps(field, taps_one, WIDE_START, WIDE_ROWS)

    def after_first(g, rows, value):
        pre = value * gain_one + bias_one
        pre_one[g, rows, :] = pre
        act = pre / (1.0 + jnp.exp(-pre))
        act = jnp.where(raw[g, rows, :] < 512.0, act, 0.0)
        hidden[g, rows, :] = act.astype(BF16).astype(F32)

    convolve(taps_one, 0, WIDE_START, WIDE_ROWS, after_first)

    gather_taps(hidden, taps_two, OWN_START, OWN_ROWS)

    def after_second(g, rows, value):
        pre = value * gain_two + bias_two + field[g, rows, :]
        s = 1.0 / (1.0 + jnp.exp(-pre))
        hidden[g, rows, :] = pre * s
        d = cot[g, rows, :] * (s + pre * s * (1.0 - s))
        d_two[g, rows, :] = d
        e_two[g, rows, :] = (d * gain_two).astype(BF16).astype(F32)

    convolve(taps_two, 1, OWN_START, OWN_ROWS, after_second)

    pack(e_two, 1)
    start(1)
    own = slice(BASE + OWN_START, BASE + OWN_START + OWN_ROWS)
    for g in range(GROUPS):
        turned[g * LANES : (g + 1) * LANES, :] = jnp.transpose(e_two[g, own, :]).astype(BF16)
    weight_gradient(taps_two, 0, 1)
    collect(hidden, out_ref)
    finish(1)
    unpack(e_two, 1)

    gather_taps(e_two, taps_back, WIDE_START, WIDE_ROWS)

    def after_third(g, rows, value):
        pre = pre_one[g, rows, :]
        s = 1.0 / (1.0 + jnp.exp(-pre))
        e = value * (s + pre * s * (1.0 - s)) * gain_one
        e = jnp.where(raw[g, rows, :] < 512.0, e, 0.0)
        e_one[g, rows, :] = e.astype(BF16).astype(F32)

    convolve(taps_back, 2, WIDE_START, WIDE_ROWS, after_third)

    gather_taps(e_one, taps_back, OWN_START, OWN_ROWS)

    def after_fourth(g, rows, value):
        d_two[g, rows, :] = d_two[g, rows, :] + value

    convolve(taps_back, 3, OWN_START, OWN_ROWS, after_fourth)
    collect(d_two, grad_ref)
    y_cell = lax.rem(lax.broadcasted_iota(jnp.int32, (OWN_ROWS, LANES), 0), YS)
    inside = (y_cell >= HALO) & (y_cell < HALO + Y)
    for g in range(GROUPS):
        turned[g * LANES : (g + 1) * LANES, :] = jnp.transpose(
            jnp.where(inside, e_one[g, own, :], 0.0)
        ).astype(BF16)
    weight_gradient(taps_one, OWN_START - WIDE_START, 0)


def per_device(
    tiles_x,
    voxels,
    features,
    cotangent,
    positions,
    weight_first,
    weight_second,
    gain_first,
    bias_first,
    gain_second,
    bias_second,
):
    slot_pos = positions[0]
    matches = jnp.arange(NPOS, dtype=jnp.int32)[:, None] == slot_pos[None, :]
    slot_index = jnp.sum(jnp.where(matches, jnp.arange(NB, dtype=jnp.int32)[None, :], 0), axis=1)
    slot_of = jnp.where(jnp.any(matches, axis=1), slot_index, NB).astype(jnp.int32)

    def to_rows(compact, empty):
        blocks = compact[0].reshape(C, NB, BS * BS, BS).transpose(1, 2, 3, 0)
        blocks = blocks.reshape(NB, BS * BS, BS * C)
        return jnp.concatenate([blocks, jnp.full((1, BS * BS, BS * C), empty, BF16)], axis=0)

    def from_rows(blocks):
        result = blocks.reshape(NB, BS * BS, BS, C).transpose(3, 0, 1, 2)
        return result.reshape(1, C, NB, BS**3)

    def forward(weight):
        return jnp.tile(weight.transpose(0, 2, 1), (1, 1, 4))

    def backward(weight):
        return jnp.tile(weight[::-1], (1, 1, 4))

    weights = jnp.stack(
        [
            forward(weight_first),
            forward(weight_second),
            backward(weight_second),
            backward(weight_first),
        ]
    )
    scales = jnp.tile(jnp.stack([gain_first, bias_first, gain_second, bias_second]), (1, 4))
    grid = pltpu.VMEM((GROUPS, TOTAL, LANES), F32)
    smem = pl.BlockSpec(memory_space=pltpu.SMEM)
    vmem = pl.BlockSpec(memory_space=pltpu.VMEM)
    block_output, block_grad, wgrad = pl.pallas_call(
        functools.partial(kernel, tiles_x),
        out_shape=(
            jax.ShapeDtypeStruct((NB, BS * BS, BS * C), BF16),
            jax.ShapeDtypeStruct((NB, BS * BS, BS * C), BF16),
            jax.ShapeDtypeStruct((2, 27, C, LANES), F32),
        ),
        in_specs=[smem, smem, vmem, vmem, vmem, vmem],
        out_specs=(vmem, vmem, vmem),
        scratch_shapes=[
            grid,
            grid,
            grid,
            grid,
            grid,
            grid,
            grid,
            grid,
            pltpu.VMEM((2, TOTAL, LANES), F32),
            pltpu.VMEM((2, WIDE_ROWS, 9 * 256), BF16),
            pltpu.VMEM((2, OWN_ROWS, 9 * 256), BF16),
            pltpu.VMEM((2, WIDE_ROWS, 9 * 256), BF16),
            pltpu.VMEM((WIDE_ROWS, 5 * LANES), BF16),
            pltpu.VMEM((4, 9 * 256, 256), BF16),
            pltpu.VMEM((4, 5 * LANES, 256), BF16),
            pltpu.VMEM((GROUPS * LANES, OWN_ROWS), BF16),
            pltpu.VMEM((NPOS + 1, BS * BS, BS * C), BF16),
            pltpu.VMEM((2, 2, HALO * Y, 512), BF16),
            pltpu.VMEM((2, 2, HALO * X, 512), BF16),
            pltpu.VMEM((2, 4, 16, 512), BF16),
            pltpu.VMEM((2, 2, HALO * Y, 512), BF16),
            pltpu.VMEM((2, 2, HALO * X, 512), BF16),
            pltpu.VMEM((2, 4, 16, 512), BF16),
            pltpu.SemaphoreType.DMA((2, 8)),
            pltpu.SemaphoreType.DMA((2, 8)),
        ],
        compiler_params=pltpu.CompilerParams(
            collective_id=0, has_side_effects=True, vmem_limit_bytes=60 * 1024 * 1024
        ),
    )(slot_of, slot_pos, to_rows(features, EMPTY), to_rows(cotangent, 0.0), weights, scales)
    local = wgrad[:, :, :, :C] * (1.0 / jnp.sqrt(jnp.float32(voxels)))
    summed = lax.psum(local, ("tile", "rep"))
    return from_rows(block_output), from_rows(block_grad), summed[0], summed[1]


def solution(mesh):
    split = P("rep", None, "tile", None)
    tiles, regions = mesh.shape["tile"], mesh.shape["rep"]
    return jax.shard_map(
        functools.partial(per_device, tiles // TGY, tiles * regions * NB * BS**3),
        mesh=mesh,
        in_specs=(split, split, P("rep", "tile"), P(), P(), P(), P(), P(), P()),
        out_specs=(split, split, P(), P()),
        check_vma=False,
    )
```

```python
import functools

import jax
import jax.numpy as jnp
from jax import lax
from jax.experimental import pallas as pl
from jax.experimental.pallas import tpu as pltpu
from jax.sharding import PartitionSpec as P

BS = 8
PX = 4
PY = 2
PZ = 2
TGY = 4
C = 32
X = PX * BS
Y = PY * BS
NPOS = PX * PY * PZ
NB = 8
HALO = 2
YS = Y + 2 * HALO
ROWS = (X + 2 * HALO) * YS
BASE = 16
TOTAL = BASE + ROWS + 16
WIDE_START, WIDE_ROWS = 8, 704
OWN_START, OWN_ROWS = HALO * YS, X * YS
EMPTY = 1024.0
SUM_ROWS = 256
GROUPS = 4
LANES = 128
F32 = jnp.float32
BF16 = jnp.bfloat16
MESH = pl.DeviceIdType.MESH
SHIFTS = [(t // 3 - 1) * YS + (t % 3 - 1) for t in range(9)]
WAYS = [(-1, 0), (1, 0), (0, -1), (0, 1), (-1, -1), (-1, 1), (1, -1), (1, 1)]


def first_cell(way, extent):
    return HALO if way < 0 else extent


def landing_cell(way, extent):
    return HALO + extent if way < 0 else 0


def kernel(
    tiles,
    regions,
    scale,
    positions,
    feats,
    cots,
    weight_first,
    weight_second,
    gain_first,
    bias_first,
    gain_second,
    bias_second,
    out_ref,
    grad_ref,
    wgrad_first,
    wgrad_second,
    raw,
    field,
    pre_one,
    hidden,
    cot,
    d_two,
    e_two,
    e_one,
    edge,
    taps_one,
    taps_two,
    taps_back,
    corner_taps,
    band,
    band_corner,
    turned,
    staged,
    send_x,
    send_y,
    send_c,
    recv_x,
    recv_y,
    recv_c,
    flat,
    spun,
    blocks,
    sums,
    scattered,
    parts,
    totals,
    send_sem,
    recv_sem,
    scatter_send,
    scatter_recv,
    part_send,
    part_recv,
    total_send,
    total_recv,
):
    me = lax.axis_index("tile")
    rep_me = lax.axis_index("rep")
    tiles_x = tiles // TGY
    piece = SUM_ROWS // tiles
    tx = me // TGY
    ty = me % TGY

    def exists(way, sign):
        ix, iy = tx + sign * way[0], ty + sign * way[1]
        return (ix >= 0) & (ix < tiles_x) & (iy >= 0) & (iy < TGY)

    def partner(way, sign):
        return me + sign * (way[0] * TGY + way[1])

    recv_x[0] = jnp.full(recv_x.shape[1:], EMPTY, BF16)
    recv_y[0] = jnp.full(recv_y.shape[1:], EMPTY, BF16)
    recv_c[0] = jnp.full(recv_c.shape[1:], EMPTY, BF16)
    recv_x[1] = jnp.zeros(recv_x.shape[1:], BF16)
    recv_y[1] = jnp.zeros(recv_y.shape[1:], BF16)
    recv_c[1] = jnp.zeros(recv_c.shape[1:], BF16)

    barrier = pltpu.get_barrier_semaphore()
    for k in range(1, tiles):
        pl.semaphore_signal(
            barrier, inc=1, device_id={"tile": lax.rem(me + k, tiles)}, device_id_type=MESH
        )
    for k in range(1, regions):
        pl.semaphore_signal(
            barrier, inc=1, device_id={"rep": lax.rem(rep_me + k, regions)}, device_id_type=MESH
        )

    def buffers(which, number):
        if number < 2:
            return send_x.at[which, number], recv_x.at[which, number]
        if number < 4:
            return send_y.at[which, number - 2], recv_y.at[which, number - 2]
        return send_c.at[which, number - 4], recv_c.at[which, number - 4]

    def transfer(which, number, sign):
        source, target = buffers(which, number)
        return pltpu.make_async_remote_copy(
            src_ref=source,
            dst_ref=target,
            send_sem=send_sem.at[which, number],
            recv_sem=recv_sem.at[which, number],
            device_id={"tile": partner(WAYS[number], sign)},
            device_id_type=MESH,
        )

    def pack(grid, which):
        for number, (wx, wy) in enumerate(WAYS):
            for g in range(GROUPS):
                lanes = slice(g * LANES, (g + 1) * LANES)
                if number < 2:
                    for k in range(HALO):
                        row = BASE + (first_cell(wx, X) + k) * YS + HALO
                        send_x[which, number, k * Y : (k + 1) * Y, lanes] = grid[
                            g, row : row + Y, :
                        ].astype(BF16)
                elif number < 4:
                    for k in range(HALO):
                        row = BASE + OWN_START + first_cell(wy, Y) + k
                        send_y[which, number - 2, k * X : (k + 1) * X, lanes] = grid[
                            g, pl.ds(row, X, stride=YS), :
                        ].astype(BF16)
                else:
                    row = BASE + first_cell(wx, X) * YS + first_cell(wy, Y)
                    both = [grid[g, row + k * YS : row + k * YS + 8, :] for k in range(HALO)]
                    send_c[which, number - 4, :, lanes] = jnp.concatenate(both, 0).astype(BF16)

    def start(which):
        for number, way in enumerate(WAYS):
            @pl.when(exists(way, 1))
            def _():
                transfer(which, number, 1).start()

    def finish(which):
        for number, way in enumerate(WAYS):
            @pl.when(exists(way, 1))
            def _():
                transfer(which, number, 1).wait_send()

            @pl.when(exists(way, -1))
            def _():
                transfer(which, number, -1).wait_recv()

    def unpack(grid, which):
        for number, (wx, wy) in enumerate(WAYS):
            for g in range(GROUPS):
                lanes = slice(g * LANES, (g + 1) * LANES)
                if number < 2:
                    for k in range(HALO):
                        row = BASE + (landing_cell(wx, X) + k) * YS + HALO
                        grid[g, row : row + Y, :] = recv_x[
                            which, number, k * Y : (k + 1) * Y, lanes
                        ].astype(F32)
                elif number < 4:
                    for k in range(HALO):
                        row = BASE + OWN_START + landing_cell(wy, Y) + k
                        grid[g, pl.ds(row, X, stride=YS), :] = recv_y[
                            which, number - 2, k * X : (k + 1) * X, lanes
                        ].astype(F32)
                else:
                    both = recv_c[which, number - 4, :, lanes].astype(F32)
                    for k in range(HALO):
                        row = BASE + (landing_cell(wx, X) + k) * YS + landing_cell(wy, Y)
                        grid[g, row : row + HALO, :] = both[k * 8 : k * 8 + HALO]

    def block_rows(p, i):
        px, py = p // (PY * PZ), p // PZ % PY
        return BASE + (HALO + px * BS + i) * YS + HALO + py * BS

    lane_group = lax.broadcasted_iota(jnp.int32, (C, LANES), 1) // C
    tall_group = lax.broadcasted_iota(jnp.int32, (BS * BS, LANES), 1) // C
    copies = (
        lax.broadcasted_iota(jnp.int32, (C, LANES), 1) % C
        == lax.broadcasted_iota(jnp.int32, (C, LANES), 0)
    ).astype(F32).astype(BF16)

    def slot_at(p):
        slot = NB
        for s in range(NB):
            slot = jnp.where(positions[0, s] == p, s, slot)
        return slot

    slots = [slot_at(p) for p in range(NPOS)]

    def spread(source, grid, empty):
        for g in range(GROUPS):
            flat[g] = source[:, g * LANES : (g + 1) * LANES].astype(F32)
        for s in range(NB):
            for g in range(GROUPS):
                part = flat[g, pl.ds(s, C, stride=NB), :].astype(BF16)
                spun[s, g * LANES : (g + 1) * LANES, :] = lax.dot_general(
                    part, copies, (((0,), (0,)), ((), ())), preferred_element_type=F32
                )
            for half in range(2):
                total = spun[s, pl.ds(half * 4, BS * BS, stride=BS), :]
                for k in range(1, 4):
                    other = spun[s, pl.ds(half * 4 + k, BS * BS, stride=BS), :]
                    total = jnp.where(tall_group == k, other, total)
                blocks[s, :, half * LANES : (half + 1) * LANES] = total
        blocks[NB] = jnp.full(blocks.shape[1:], empty, F32)
        for p in range(NPOS):
            block = blocks[slots[p]]
            for i in range(BS):
                row = block_rows(p, i)
                for half in range(2):
                    grid[p % PZ * 2 + half, row : row + BS, :] = block[
                        i * BS : (i + 1) * BS, half * LANES : (half + 1) * LANES
                    ]

    def collect(grid, result):
        staged[NPOS] = jnp.zeros(staged.shape[1:], F32)
        for p in range(NPOS):
            for half in range(2):
                for i in range(BS):
                    row = block_rows(p, i)
                    staged[p, i * BS : (i + 1) * BS, half * LANES : (half + 1) * LANES] = grid[
                        p % PZ * 2 + half, row : row + BS, :
                    ]
        for s in range(NB):
            block = staged[positions[0, s]]
            for k in range(BS):
                part = block[:, k // 4 * LANES : (k // 4 + 1) * LANES]
                spun[s, pl.ds(k, BS * BS, stride=BS), :] = jnp.where(
                    tall_group == k % 4, part, 0.0
                )
            for g in range(GROUPS):
                flat[g, pl.ds(s, C, stride=NB), :] = lax.dot_general(
                    copies,
                    spun[s, g * LANES : (g + 1) * LANES, :].astype(BF16),
                    (((1,), (1,)), ((), ())),
                    preferred_element_type=F32,
                )
        for g in range(GROUPS):
            result[:, g * LANES : (g + 1) * LANES] = flat[g].astype(BF16)

    def scatter_copy(w, k):
        peer = lax.rem(me + k, tiles)
        return pltpu.make_async_remote_copy(
            src_ref=sums.at[w, pl.ds(pl.multiple_of(peer * piece, 8), piece), :],
            dst_ref=scattered.at[w, k],
            send_sem=scatter_send.at[w, k],
            recv_sem=scatter_recv.at[w, k],
            device_id={"tile": peer},
            device_id_type=MESH,
        )

    def part_copy(w, k):
        return pltpu.make_async_remote_copy(
            src_ref=parts.at[w, rep_me],
            dst_ref=parts.at[w, rep_me],
            send_sem=part_send.at[w, k],
            recv_sem=part_recv.at[w, k],
            device_id={"rep": lax.rem(rep_me + k, regions)},
            device_id_type=MESH,
        )

    own_piece = pl.ds(pl.multiple_of(me * piece, 8), piece)

    def total_copy(w, k):
        return pltpu.make_async_remote_copy(
            src_ref=totals.at[w, own_piece, :],
            dst_ref=totals.at[w, own_piece, :],
            send_sem=total_send.at[w, k],
            recv_sem=total_recv.at[w, k],
            device_id={"tile": lax.rem(me + k, tiles)},
            device_id_type=MESH,
        )

    def scatter_start(w):
        for k in range(1, tiles):
            scatter_copy(w, k).start()

    def scatter_finish(w):
        total = sums[w, own_piece, :]
        for k in range(1, tiles):
            scatter_copy(w, k).wait()
            total = total + scattered[w, k]
        parts[w, rep_me] = total * scale
        for k in range(1, regions):
            part_copy(w, k).start()

    def part_finish(w):
        for k in range(1, regions):
            part_copy(w, k).wait()
        total = parts[w, 0]
        for r in range(1, regions):
            total = total + parts[w, r]
        totals[w, own_piece, :] = total
        for k in range(1, tiles):
            total_copy(w, k).start()

    def total_finish(w, result):
        for k in range(1, tiles):
            total_copy(w, k).wait()
        for q in range(27):
            block = totals[w, q // 4 * C : (q // 4 + 1) * C, :]
            if q % 4:
                block = pltpu.roll(block, LANES - q % 4 * C, 1)
            result[q] = block[:, :C]

    for g in range(GROUPS):
        raw[g] = jnp.full((TOTAL, LANES), EMPTY, F32)
        cot[g] = jnp.zeros((TOTAL, LANES), F32)
        e_two[g] = jnp.zeros((TOTAL, LANES), F32)
    spread(feats, raw, EMPTY)
    pack(raw, 0)
    pl.semaphore_wait(barrier, tiles + regions - 2)
    start(0)

    picks = [(lane_group == k).astype(F32).astype(BF16) for k in range(4)]
    for w in range(4):
        band_corner[w] = jnp.zeros(band_corner.shape[1:], BF16)

    def turned_weight(ref, q):
        block = lax.dot_general(
            ref[q], copies, (((0,), (0,)), ((), ())), preferred_element_type=F32
        )
        return block.astype(BF16)

    def plain_weight(ref, q):
        return jnp.dot(ref[26 - q], copies, preferred_element_type=F32).astype(BF16)

    def build_one(w, ref, read, t):
        three = [read(ref, t * 3 + k) for k in range(3)]
        row = pl.multiple_of(t * 256, 256)
        for z_in in range(8):
            for tile in range(2):
                total = None
                for k in range(4):
                    dz = z_in - (tile * 4 + k)
                    if abs(dz) <= 1:
                        term = three[dz + 1] * picks[k]
                        total = term if total is None else total + term
                if total is None:
                    total = jnp.zeros((C, LANES), BF16)
                band[w, pl.ds(row + z_in * C, C), tile * LANES : (tile + 1) * LANES] = total
        edge_row = pl.multiple_of(t * 64, 64)
        band_corner[w, pl.ds(edge_row, C), LANES:] = three[0] * picks[0]
        band_corner[w, pl.ds(edge_row + C, C), :LANES] = three[2] * picks[3]

    def build(t, carry):
        build_one(0, weight_first, turned_weight, t)
        build_one(1, weight_second, turned_weight, t)
        build_one(2, weight_second, plain_weight, t)
        build_one(3, weight_first, plain_weight, t)
        return carry

    lax.fori_loop(0, 9, build, 0)
    spread(cots, cot, 0.0)

    def gather_taps(grid, taps, first, rows):
        lane = lax.broadcasted_iota(jnp.int32, (TOTAL, LANES), 1)
        pair = jnp.where(
            lane < C,
            pltpu.roll(grid[1], C, 1),
            jnp.where(lane < 2 * C, pltpu.roll(grid[2], C, 1), 0.0),
        )
        edge[0] = pair
        edge[1] = pltpu.roll(pair, 2 * C, 1)
        for t in range(9):
            begin = BASE + first + SHIFTS[t]
            for g in range(GROUPS):
                lanes = slice(t * 256 + g % 2 * LANES, t * 256 + g % 2 * LANES + LANES)
                taps[g // 2, :rows, lanes] = grid[g, begin : begin + rows, :].astype(BF16)
        for j in range(5):
            begin = BASE + first + SHIFTS[2 * j]
            value = edge[0, begin : begin + rows, :]
            if j < 4:
                begin = BASE + first + SHIFTS[2 * j + 1]
                value = value + edge[1, begin : begin + rows, :]
            corner_taps[:rows, j * LANES : (j + 1) * LANES] = value.astype(BF16)

    def convolve(taps, w, first, rows, finish_group):
        chunk = rows // 2

        def step(c, carry):
            here = pl.ds(pl.multiple_of(c * chunk, 16), chunk)
            low = jnp.dot(taps[0, here, :], band[w], preferred_element_type=F32)
            high = jnp.dot(taps[1, here, :], band[w], preferred_element_type=F32)
            mid = jnp.dot(corner_taps[here, :], band_corner[w], preferred_element_type=F32)
            there = pl.ds(pl.multiple_of(BASE + first + c * chunk, 8), chunk)
            finish_group(0, there, low[:, :LANES])
            finish_group(1, there, low[:, LANES:] + mid[:, :LANES])
            finish_group(2, there, high[:, :LANES] + mid[:, LANES:])
            finish_group(3, there, high[:, LANES:])
            return carry

        lax.fori_loop(0, 2, step, 0)

    def weight_gradient(taps, offset, which):
        def step(t, carry):
            lanes = pl.ds(pl.multiple_of(t * 256, 256), 256)
            products = [
                jnp.dot(
                    turned[half * 224 : half * 224 + 288, :],
                    taps[half, offset : offset + OWN_ROWS, lanes],
                    preferred_element_type=F32,
                )
                for half in range(2)
            ]
            for dz in range(-1, 2):
                total = jnp.zeros((C, LANES), F32)
                for half in range(2):
                    for b in range(8):
                        a = b + half - dz
                        if 0 <= a <= 8:
                            part = products[half][
                                a * C : (a + 1) * C, b // 4 * LANES : (b // 4 + 1) * LANES
                            ]
                            total = total + jnp.where(lane_group == b % 4, part, 0.0)
                total = total + pltpu.roll(total, 64, 1)
                total = total + pltpu.roll(total, 32, 1)
                q = t * 3 + (dz + 1)
                rows = pl.ds(pl.multiple_of(lax.div(q, 4) * C, C), C)
                sums[which, rows, :] += jnp.where(lane_group == lax.rem(q, 4), total, 0.0)
            return carry

        lax.fori_loop(0, 9, step, 0)

    def wide(ref):
        return jnp.concatenate([ref[...]] * 4, axis=1)

    sums[...] = jnp.zeros(sums.shape, F32)
    gain_one, bias_one = wide(gain_first), wide(bias_first)
    gain_two, bias_two = wide(gain_second), wide(bias_second)

    finish(0)
    unpack(raw, 0)
    for g in range(GROUPS):
        value = raw[g]
        field[g] = jnp.where(value < 512.0, value, 0.0)

    gather_taps(field, taps_one, WIDE_START, WIDE_ROWS)

    def after_first(g, rows, value):
        pre = value * gain_one + bias_one
        pre_one[g, rows, :] = pre
        act = pre / (1.0 + jnp.exp(-pre))
        act = jnp.where(raw[g, rows, :] < 512.0, act, 0.0)
        hidden[g, rows, :] = act.astype(BF16).astype(F32)

    convolve(taps_one, 0, WIDE_START, WIDE_ROWS, after_first)

    gather_taps(hidden, taps_two, OWN_START, OWN_ROWS)

    def after_second(g, rows, value):
        pre = value * gain_two + bias_two + field[g, rows, :]
        s = 1.0 / (1.0 + jnp.exp(-pre))
        hidden[g, rows, :] = pre * s
        d = cot[g, rows, :] * (s + pre * s * (1.0 - s))
        d_two[g, rows, :] = d
        e_two[g, rows, :] = (d * gain_two).astype(BF16).astype(F32)

    convolve(taps_two, 1, OWN_START, OWN_ROWS, after_second)

    pack(e_two, 1)
    start(1)
    own = slice(BASE + OWN_START, BASE + OWN_START + OWN_ROWS)
    for g in range(GROUPS):
        turned[g * LANES : (g + 1) * LANES, :] = jnp.transpose(e_two[g, own, :]).astype(BF16)
    weight_gradient(taps_two, 0, 1)
    scatter_start(1)
    collect(hidden, out_ref)
    finish(1)
    unpack(e_two, 1)

    gather_taps(e_two, taps_back, WIDE_START, WIDE_ROWS)

    def after_third(g, rows, value):
        pre = pre_one[g, rows, :]
        s = 1.0 / (1.0 + jnp.exp(-pre))
        e = value * (s + pre * s * (1.0 - s)) * gain_one
        e = jnp.where(raw[g, rows, :] < 512.0, e, 0.0)
        e_one[g, rows, :] = e.astype(BF16).astype(F32)

    convolve(taps_back, 2, WIDE_START, WIDE_ROWS, after_third)

    scatter_finish(1)
    y_cell = lax.rem(lax.broadcasted_iota(jnp.int32, (OWN_ROWS, LANES), 0), YS)
    inside = (y_cell >= HALO) & (y_cell < HALO + Y)
    for g in range(GROUPS):
        turned[g * LANES : (g + 1) * LANES, :] = jnp.transpose(
            jnp.where(inside, e_one[g, own, :], 0.0)
        ).astype(BF16)
    weight_gradient(taps_one, OWN_START - WIDE_START, 0)
    scatter_start(0)
    part_finish(1)

    gather_taps(e_one, taps_back, OWN_START, OWN_ROWS)
    scatter_finish(0)

    def after_fourth(g, rows, value):
        d_two[g, rows, :] = d_two[g, rows, :] + value

    convolve(taps_back, 3, OWN_START, OWN_ROWS, after_fourth)
    part_finish(0)
    collect(d_two, grad_ref)
    total_finish(1, wgrad_second)
    total_finish(0, wgrad_first)


def per_device(
    tiles,
    regions,
    features,
    cotangent,
    positions,
    weight_first,
    weight_second,
    gain_first,
    bias_first,
    gain_second,
    bias_second,
):
    def flatten(array):
        return array.reshape(C * NB, BS**3)

    def row(vector):
        return vector.reshape(1, C)

    scale = 1.0 / float(tiles * regions * NB * BS**3) ** 0.5
    piece = SUM_ROWS // tiles
    grid = pltpu.VMEM((GROUPS, TOTAL, LANES), F32)
    smem = pl.BlockSpec(memory_space=pltpu.SMEM)
    vmem = pl.BlockSpec(memory_space=pltpu.VMEM)
    block_output, block_grad, grad_first, grad_second = pl.pallas_call(
        functools.partial(kernel, tiles, regions, scale),
        out_shape=(
            jax.ShapeDtypeStruct((C * NB, BS**3), BF16),
            jax.ShapeDtypeStruct((C * NB, BS**3), BF16),
            jax.ShapeDtypeStruct((27, C, C), F32),
            jax.ShapeDtypeStruct((27, C, C), F32),
        ),
        in_specs=[smem] + [vmem] * 8,
        out_specs=(vmem, vmem, vmem, vmem),
        scratch_shapes=[
            grid,
            grid,
            grid,
            grid,
            grid,
            grid,
            grid,
            grid,
            pltpu.VMEM((2, TOTAL, LANES), F32),
            pltpu.VMEM((2, WIDE_ROWS, 9 * 256), BF16),
            pltpu.VMEM((2, OWN_ROWS, 9 * 256), BF16),
            pltpu.VMEM((2, WIDE_ROWS, 9 * 256), BF16),
            pltpu.VMEM((WIDE_ROWS, 5 * LANES), BF16),
            pltpu.VMEM((4, 9 * 256, 256), BF16),
            pltpu.VMEM((4, 5 * LANES, 256), BF16),
            pltpu.VMEM((GROUPS * LANES, OWN_ROWS), BF16),
            pltpu.VMEM((NPOS + 1, BS * BS, BS * C), F32),
            pltpu.VMEM((2, 2, HALO * Y, 512), BF16),
            pltpu.VMEM((2, 2, HALO * X, 512), BF16),
            pltpu.VMEM((2, 4, 16, 512), BF16),
            pltpu.VMEM((2, 2, HALO * Y, 512), BF16),
            pltpu.VMEM((2, 2, HALO * X, 512), BF16),
            pltpu.VMEM((2, 4, 16, 512), BF16),
            pltpu.VMEM((GROUPS, C * NB, LANES), F32),
            pltpu.VMEM((NB, BS**3, LANES), F32),
            pltpu.VMEM((NB + 1, BS * BS, BS * C), F32),
            pltpu.VMEM((2, SUM_ROWS, LANES), F32),
            pltpu.VMEM((2, tiles, piece, LANES), F32),
            pltpu.VMEM((2, regions, piece, LANES), F32),
            pltpu.VMEM((2, SUM_ROWS, LANES), F32),
            pltpu.SemaphoreType.DMA((2, 8)),
            pltpu.SemaphoreType.DMA((2, 8)),
            pltpu.SemaphoreType.DMA((2, tiles)),
            pltpu.SemaphoreType.DMA((2, tiles)),
            pltpu.SemaphoreType.DMA((2, regions)),
            pltpu.SemaphoreType.DMA((2, regions)),
            pltpu.SemaphoreType.DMA((2, tiles)),
            pltpu.SemaphoreType.DMA((2, tiles)),
        ],
        compiler_params=pltpu.CompilerParams(
            collective_id=0, has_side_effects=True, vmem_limit_bytes=60 * 1024 * 1024
        ),
    )(
        positions,
        flatten(features),
        flatten(cotangent),
        weight_first,
        weight_second,
        row(gain_first),
        row(bias_first),
        row(gain_second),
        row(bias_second),
    )
    shape = (1, C, NB, BS**3)
    return block_output.reshape(shape), block_grad.reshape(shape), grad_first, grad_second


def solution(mesh):
    split = P("rep", None, "tile", None)
    tiles, regions = mesh.shape["tile"], mesh.shape["rep"]
    return jax.shard_map(
        functools.partial(per_device, tiles, regions),
        mesh=mesh,
        in_specs=(split, split, P("rep", "tile"), P(), P(), P(), P(), P(), P()),
        out_specs=(split, split, P(), P()),
        check_vma=False,
    )
```

```python
import functools

import jax
import jax.numpy as jnp
from jax import lax
from jax.experimental import pallas as pl
from jax.experimental.pallas import tpu as pltpu
from jax.sharding import PartitionSpec as P

BS = 8
PX = 4
PY = 2
PZ = 2
TGY = 4
C = 32
X = PX * BS
Y = PY * BS
NPOS = PX * PY * PZ
NB = 8
HALO = 2
YS = Y + 2 * HALO
ROWS = (X + 2 * HALO) * YS
BASE = 16
TOTAL = BASE + ROWS + 16
WIDE_START, WIDE_ROWS = 8, 704
OWN_START, OWN_ROWS = HALO * YS, X * YS
EMPTY = 1024.0
SUM_ROWS = 256
GROUPS = 4
LANES = 128
F32 = jnp.float32
BF16 = jnp.bfloat16
MESH = pl.DeviceIdType.MESH
SHIFTS = [(t // 3 - 1) * YS + (t % 3 - 1) for t in range(9)]
WAYS = [(-1, 0), (1, 0), (0, -1), (0, 1), (-1, -1), (-1, 1), (1, -1), (1, 1)]


def first_cell(way, extent):
    return HALO if way < 0 else extent


def landing_cell(way, extent):
    return HALO + extent if way < 0 else 0


def sigmoid(values):
    return 0.5 + 0.5 * jnp.tanh(0.5 * values)


def kernel(
    tiles,
    regions,
    scale,
    positions,
    feats,
    cots,
    weight_first,
    weight_second,
    gain_first,
    bias_first,
    gain_second,
    bias_second,
    out_ref,
    grad_ref,
    wgrad_first,
    wgrad_second,
    raw,
    field,
    slope_one,
    hidden,
    cot,
    d_two,
    e_two,
    e_one,
    edge,
    taps_one,
    taps_two,
    taps_back,
    corner_taps,
    band,
    band_corner,
    turned,
    staged,
    send_x,
    send_y,
    send_c,
    recv_x,
    recv_y,
    recv_c,
    flat,
    spun,
    blocks,
    sums,
    scattered,
    parts,
    totals,
    send_sem,
    recv_sem,
    scatter_send,
    scatter_recv,
    part_send,
    part_recv,
    total_send,
    total_recv,
):
    me = lax.axis_index("tile")
    rep_me = lax.axis_index("rep")
    tiles_x = tiles // TGY
    piece = SUM_ROWS // tiles
    tx = me // TGY
    ty = me % TGY

    def exists(way, sign):
        ix, iy = tx + sign * way[0], ty + sign * way[1]
        return (ix >= 0) & (ix < tiles_x) & (iy >= 0) & (iy < TGY)

    def partner(way, sign):
        return me + sign * (way[0] * TGY + way[1])

    recv_x[0] = jnp.full(recv_x.shape[1:], EMPTY, BF16)
    recv_y[0] = jnp.full(recv_y.shape[1:], EMPTY, BF16)
    recv_c[0] = jnp.full(recv_c.shape[1:], EMPTY, BF16)
    recv_x[1] = jnp.zeros(recv_x.shape[1:], BF16)
    recv_y[1] = jnp.zeros(recv_y.shape[1:], BF16)
    recv_c[1] = jnp.zeros(recv_c.shape[1:], BF16)

    barrier = pltpu.get_barrier_semaphore()
    for k in range(1, tiles):
        pl.semaphore_signal(
            barrier, inc=1, device_id={"tile": lax.rem(me + k, tiles)}, device_id_type=MESH
        )
    for k in range(1, regions):
        pl.semaphore_signal(
            barrier, inc=1, device_id={"rep": lax.rem(rep_me + k, regions)}, device_id_type=MESH
        )

    def buffers(which, number):
        if number < 2:
            return send_x.at[which, number], recv_x.at[which, number]
        if number < 4:
            return send_y.at[which, number - 2], recv_y.at[which, number - 2]
        return send_c.at[which, number - 4], recv_c.at[which, number - 4]

    def transfer(which, number, sign):
        source, target = buffers(which, number)
        return pltpu.make_async_remote_copy(
            src_ref=source,
            dst_ref=target,
            send_sem=send_sem.at[which, number],
            recv_sem=recv_sem.at[which, number],
            device_id={"tile": partner(WAYS[number], sign)},
            device_id_type=MESH,
        )

    def pack(grid, which):
        for number, (wx, wy) in enumerate(WAYS):
            for g in range(GROUPS):
                lanes = slice(g * LANES, (g + 1) * LANES)
                if number < 2:
                    for k in range(HALO):
                        row = BASE + (first_cell(wx, X) + k) * YS + HALO
                        send_x[which, number, k * Y : (k + 1) * Y, lanes] = grid[
                            g, row : row + Y, :
                        ].astype(BF16)
                elif number < 4:
                    for k in range(HALO):
                        row = BASE + OWN_START + first_cell(wy, Y) + k
                        send_y[which, number - 2, k * X : (k + 1) * X, lanes] = grid[
                            g, pl.ds(row, X, stride=YS), :
                        ].astype(BF16)
                else:
                    row = BASE + first_cell(wx, X) * YS + first_cell(wy, Y)
                    both = [grid[g, row + k * YS : row + k * YS + 8, :] for k in range(HALO)]
                    send_c[which, number - 4, :, lanes] = jnp.concatenate(both, 0).astype(BF16)

    def start(which):
        for number, way in enumerate(WAYS):
            @pl.when(exists(way, 1))
            def _():
                transfer(which, number, 1).start()

    def finish(which):
        for number, way in enumerate(WAYS):
            @pl.when(exists(way, 1))
            def _():
                transfer(which, number, 1).wait_send()

            @pl.when(exists(way, -1))
            def _():
                transfer(which, number, -1).wait_recv()

    def unpack(grid, which):
        for number, (wx, wy) in enumerate(WAYS):
            for g in range(GROUPS):
                lanes = slice(g * LANES, (g + 1) * LANES)
                if number < 2:
                    for k in range(HALO):
                        row = BASE + (landing_cell(wx, X) + k) * YS + HALO
                        grid[g, row : row + Y, :] = recv_x[
                            which, number, k * Y : (k + 1) * Y, lanes
                        ].astype(F32)
                elif number < 4:
                    for k in range(HALO):
                        row = BASE + OWN_START + landing_cell(wy, Y) + k
                        grid[g, pl.ds(row, X, stride=YS), :] = recv_y[
                            which, number - 2, k * X : (k + 1) * X, lanes
                        ].astype(F32)
                else:
                    both = recv_c[which, number - 4, :, lanes].astype(F32)
                    for k in range(HALO):
                        row = BASE + (landing_cell(wx, X) + k) * YS + landing_cell(wy, Y)
                        grid[g, row : row + HALO, :] = both[k * 8 : k * 8 + HALO]

    def block_rows(p, i):
        px, py = p // (PY * PZ), p // PZ % PY
        return BASE + (HALO + px * BS + i) * YS + HALO + py * BS

    lane_group = lax.broadcasted_iota(jnp.int32, (C, LANES), 1) // C
    tall_group = lax.broadcasted_iota(jnp.int32, (BS * BS, LANES), 1) // C
    copies = (
        lax.broadcasted_iota(jnp.int32, (C, LANES), 1) % C
        == lax.broadcasted_iota(jnp.int32, (C, LANES), 0)
    ).astype(F32).astype(BF16)

    def slot_at(p):
        slot = NB
        for s in range(NB):
            slot = jnp.where(positions[0, s] == p, s, slot)
        return slot

    slots = [slot_at(p) for p in range(NPOS)]

    def spread(source, grid, empty):
        for g in range(GROUPS):
            flat[g] = source[:, g * LANES : (g + 1) * LANES].astype(F32)
        for s in range(NB):
            for g in range(GROUPS):
                part = flat[g, pl.ds(s, C, stride=NB), :].astype(BF16)
                spun[s, g * LANES : (g + 1) * LANES, :] = lax.dot_general(
                    part, copies, (((0,), (0,)), ((), ())), preferred_element_type=F32
                )
            for half in range(2):
                total = spun[s, pl.ds(half * 4, BS * BS, stride=BS), :]
                for k in range(1, 4):
                    other = spun[s, pl.ds(half * 4 + k, BS * BS, stride=BS), :]
                    total = jnp.where(tall_group == k, other, total)
                blocks[s, :, half * LANES : (half + 1) * LANES] = total
        blocks[NB] = jnp.full(blocks.shape[1:], empty, F32)
        for p in range(NPOS):
            block = blocks[slots[p]]
            for i in range(BS):
                row = block_rows(p, i)
                for half in range(2):
                    grid[p % PZ * 2 + half, row : row + BS, :] = block[
                        i * BS : (i + 1) * BS, half * LANES : (half + 1) * LANES
                    ]

    def collect(grid, result):
        staged[NPOS] = jnp.zeros(staged.shape[1:], F32)
        for p in range(NPOS):
            for half in range(2):
                for i in range(BS):
                    row = block_rows(p, i)
                    staged[p, i * BS : (i + 1) * BS, half * LANES : (half + 1) * LANES] = grid[
                        p % PZ * 2 + half, row : row + BS, :
                    ]
        for s in range(NB):
            block = staged[positions[0, s]]
            for k in range(BS):
                part = block[:, k // 4 * LANES : (k // 4 + 1) * LANES]
                spun[s, pl.ds(k, BS * BS, stride=BS), :] = jnp.where(
                    tall_group == k % 4, part, 0.0
                )
            for g in range(GROUPS):
                flat[g, pl.ds(s, C, stride=NB), :] = lax.dot_general(
                    copies,
                    spun[s, g * LANES : (g + 1) * LANES, :].astype(BF16),
                    (((1,), (1,)), ((), ())),
                    preferred_element_type=F32,
                )
        for g in range(GROUPS):
            result[:, g * LANES : (g + 1) * LANES] = flat[g].astype(BF16)

    def scatter_copy(w, k):
        peer = lax.rem(me + k, tiles)
        return pltpu.make_async_remote_copy(
            src_ref=sums.at[w, pl.ds(pl.multiple_of(peer * piece, 8), piece), :],
            dst_ref=scattered.at[w, k],
            send_sem=scatter_send.at[w, k],
            recv_sem=scatter_recv.at[w, k],
            device_id={"tile": peer},
            device_id_type=MESH,
        )

    def part_copy(w, k):
        return pltpu.make_async_remote_copy(
            src_ref=parts.at[w, rep_me],
            dst_ref=parts.at[w, rep_me],
            send_sem=part_send.at[w, k],
            recv_sem=part_recv.at[w, k],
            device_id={"rep": lax.rem(rep_me + k, regions)},
            device_id_type=MESH,
        )

    own_piece = pl.ds(pl.multiple_of(me * piece, 8), piece)

    def total_copy(w, k):
        return pltpu.make_async_remote_copy(
            src_ref=totals.at[w, own_piece, :],
            dst_ref=totals.at[w, own_piece, :],
            send_sem=total_send.at[w, k],
            recv_sem=total_recv.at[w, k],
            device_id={"tile": lax.rem(me + k, tiles)},
            device_id_type=MESH,
        )

    def scatter_start(w):
        for k in range(1, tiles):
            scatter_copy(w, k).start()

    def scatter_finish(w):
        total = sums[w, own_piece, :]
        for k in range(1, tiles):
            scatter_copy(w, k).wait()
            total = total + scattered[w, k]
        parts[w, rep_me] = total * scale
        for k in range(1, regions):
            part_copy(w, k).start()

    def part_finish(w):
        for k in range(1, regions):
            part_copy(w, k).wait()
        total = parts[w, 0]
        for r in range(1, regions):
            total = total + parts[w, r]
        totals[w, own_piece, :] = total
        for k in range(1, tiles):
            total_copy(w, k).start()

    def total_finish(w, result):
        for k in range(1, tiles):
            total_copy(w, k).wait()
        for q in range(27):
            block = totals[w, q // 4 * C : (q // 4 + 1) * C, :]
            if q % 4:
                block = pltpu.roll(block, LANES - q % 4 * C, 1)
            result[q] = block[:, :C]

    for g in range(GROUPS):
        raw[g] = jnp.full((TOTAL, LANES), EMPTY, F32)
        cot[g] = jnp.zeros((TOTAL, LANES), F32)
        e_two[g] = jnp.zeros((TOTAL, LANES), F32)
    spread(feats, raw, EMPTY)
    pack(raw, 0)
    pl.semaphore_wait(barrier, tiles + regions - 2)
    start(0)

    picks = [(lane_group == k).astype(F32).astype(BF16) for k in range(4)]
    for w in range(4):
        band_corner[w] = jnp.zeros(band_corner.shape[1:], BF16)

    def turned_weight(ref, q):
        block = lax.dot_general(
            ref[q], copies, (((0,), (0,)), ((), ())), preferred_element_type=F32
        )
        return block.astype(BF16)

    def plain_weight(ref, q):
        return jnp.dot(ref[26 - q], copies, preferred_element_type=F32).astype(BF16)

    def build_one(w, ref, read, t):
        three = [read(ref, t * 3 + k) for k in range(3)]
        row = pl.multiple_of(t * 256, 256)
        for z_in in range(8):
            for tile in range(2):
                total = None
                for k in range(4):
                    dz = z_in - (tile * 4 + k)
                    if abs(dz) <= 1:
                        term = three[dz + 1] * picks[k]
                        total = term if total is None else total + term
                if total is None:
                    total = jnp.zeros((C, LANES), BF16)
                band[w, pl.ds(row + z_in * C, C), tile * LANES : (tile + 1) * LANES] = total
        edge_row = pl.multiple_of(t * 64, 64)
        band_corner[w, pl.ds(edge_row, C), LANES:] = three[0] * picks[0]
        band_corner[w, pl.ds(edge_row + C, C), :LANES] = three[2] * picks[3]

    def build(t, carry):
        build_one(0, weight_first, turned_weight, t)
        build_one(1, weight_second, turned_weight, t)
        build_one(2, weight_second, plain_weight, t)
        build_one(3, weight_first, plain_weight, t)
        return carry

    lax.fori_loop(0, 9, build, 0)
    spread(cots, cot, 0.0)

    def gather_taps(grid, taps, first, rows):
        lane = lax.broadcasted_iota(jnp.int32, (TOTAL, LANES), 1)
        pair = jnp.where(
            lane < C,
            pltpu.roll(grid[1], C, 1),
            jnp.where(lane < 2 * C, pltpu.roll(grid[2], C, 1), 0.0),
        )
        edge[0] = pair
        edge[1] = pltpu.roll(pair, 2 * C, 1)
        for t in range(9):
            begin = BASE + first + SHIFTS[t]
            for g in range(GROUPS):
                lanes = slice(t * 256 + g % 2 * LANES, t * 256 + g % 2 * LANES + LANES)
                taps[g // 2, :rows, lanes] = grid[g, begin : begin + rows, :].astype(BF16)
        for j in range(5):
            begin = BASE + first + SHIFTS[2 * j]
            value = edge[0, begin : begin + rows, :]
            if j < 4:
                begin = BASE + first + SHIFTS[2 * j + 1]
                value = value + edge[1, begin : begin + rows, :]
            corner_taps[:rows, j * LANES : (j + 1) * LANES] = value.astype(BF16)

    def convolve(taps, w, first, rows, finish_group):
        chunk = rows // 2

        def step(c, carry):
            here = pl.ds(pl.multiple_of(c * chunk, 16), chunk)
            low = jnp.dot(taps[0, here, :], band[w], preferred_element_type=F32)
            high = jnp.dot(taps[1, here, :], band[w], preferred_element_type=F32)
            mid = jnp.dot(corner_taps[here, :], band_corner[w], preferred_element_type=F32)
            there = pl.ds(pl.multiple_of(BASE + first + c * chunk, 8), chunk)
            finish_group(0, there, low[:, :LANES])
            finish_group(1, there, low[:, LANES:] + mid[:, :LANES])
            finish_group(2, there, high[:, :LANES] + mid[:, LANES:])
            finish_group(3, there, high[:, LANES:])
            return carry

        lax.fori_loop(0, 2, step, 0)

    def weight_gradient(taps, offset, which):
        def step(x_tap, carry):
            lanes = pl.ds(pl.multiple_of(x_tap * 768, 256), 768)
            products = [
                jnp.dot(
                    turned[half * 224 : half * 224 + 288, :],
                    taps[half, offset : offset + OWN_ROWS, lanes],
                    preferred_element_type=F32,
                )
                for half in range(2)
            ]
            for y_tap in range(3):
                for dz in range(-1, 2):
                    total = jnp.zeros((C, LANES), F32)
                    for half in range(2):
                        for b in range(8):
                            a = b + half - dz
                            if 0 <= a <= 8:
                                begin = y_tap * 256 + b // 4 * LANES
                                part = products[half][a * C : (a + 1) * C, begin : begin + LANES]
                                total = total + jnp.where(lane_group == b % 4, part, 0.0)
                    total = total + pltpu.roll(total, 64, 1)
                    total = total + pltpu.roll(total, 32, 1)
                    q = x_tap * 9 + (y_tap * 3 + dz + 1)
                    rows = pl.ds(pl.multiple_of(lax.div(q, 4) * C, C), C)
                    sums[which, rows, :] += jnp.where(lane_group == lax.rem(q, 4), total, 0.0)
            return carry

        lax.fori_loop(0, 3, step, 0)

    def wide(ref):
        return jnp.concatenate([ref[...]] * 4, axis=1)

    sums[...] = jnp.zeros(sums.shape, F32)
    gain_one, bias_one = wide(gain_first), wide(bias_first)
    gain_two, bias_two = wide(gain_second), wide(bias_second)

    finish(0)
    unpack(raw, 0)
    for g in range(GROUPS):
        value = raw[g]
        field[g] = jnp.where(value < 512.0, value, 0.0)

    gather_taps(field, taps_one, WIDE_START, WIDE_ROWS)

    def after_first(g, rows, value):
        pre = value * gain_one + bias_one
        active = raw[g, rows, :] < 512.0
        s = sigmoid(pre)
        act = pre * s
        slope = (s + act * (1.0 - s)) * gain_one
        slope_one[g, rows, :] = jnp.where(active, slope, 0.0)
        hidden[g, rows, :] = jnp.where(active, act, 0.0).astype(BF16).astype(F32)

    convolve(taps_one, 0, WIDE_START, WIDE_ROWS, after_first)

    gather_taps(hidden, taps_two, OWN_START, OWN_ROWS)

    def after_second(g, rows, value):
        pre = value * gain_two + bias_two + field[g, rows, :]
        s = sigmoid(pre)
        act = pre * s
        hidden[g, rows, :] = act
        d = cot[g, rows, :] * (s + act * (1.0 - s))
        d_two[g, rows, :] = d
        e_two[g, rows, :] = (d * gain_two).astype(BF16).astype(F32)

    convolve(taps_two, 1, OWN_START, OWN_ROWS, after_second)

    pack(e_two, 1)
    start(1)
    own = slice(BASE + OWN_START, BASE + OWN_START + OWN_ROWS)
    for g in range(GROUPS):
        turned[g * LANES : (g + 1) * LANES, :] = jnp.transpose(e_two[g, own, :]).astype(BF16)
    weight_gradient(taps_two, 0, 1)
    scatter_start(1)
    collect(hidden, out_ref)
    finish(1)
    unpack(e_two, 1)

    gather_taps(e_two, taps_back, WIDE_START, WIDE_ROWS)

    def after_third(g, rows, value):
        e_one[g, rows, :] = (value * slope_one[g, rows, :]).astype(BF16).astype(F32)

    convolve(taps_back, 2, WIDE_START, WIDE_ROWS, after_third)

    scatter_finish(1)
    y_cell = lax.rem(lax.broadcasted_iota(jnp.int32, (OWN_ROWS, LANES), 0), YS)
    inside = (y_cell >= HALO) & (y_cell < HALO + Y)
    for g in range(GROUPS):
        turned[g * LANES : (g + 1) * LANES, :] = jnp.transpose(
            jnp.where(inside, e_one[g, own, :], 0.0)
        ).astype(BF16)
    weight_gradient(taps_one, OWN_START - WIDE_START, 0)
    scatter_start(0)
    part_finish(1)

    gather_taps(e_one, taps_back, OWN_START, OWN_ROWS)
    scatter_finish(0)

    def after_fourth(g, rows, value):
        d_two[g, rows, :] = d_two[g, rows, :] + value

    convolve(taps_back, 3, OWN_START, OWN_ROWS, after_fourth)
    part_finish(0)
    collect(d_two, grad_ref)
    total_finish(1, wgrad_second)
    total_finish(0, wgrad_first)


def per_device(
    tiles,
    regions,
    features,
    cotangent,
    positions,
    weight_first,
    weight_second,
    gain_first,
    bias_first,
    gain_second,
    bias_second,
):
    def flatten(array):
        return array.reshape(C * NB, BS**3)

    def row(vector):
        return vector.reshape(1, C)

    scale = 1.0 / float(tiles * regions * NB * BS**3) ** 0.5
    piece = SUM_ROWS // tiles
    grid = pltpu.VMEM((GROUPS, TOTAL, LANES), F32)
    smem = pl.BlockSpec(memory_space=pltpu.SMEM)
    vmem = pl.BlockSpec(memory_space=pltpu.VMEM)
    block_output, block_grad, grad_first, grad_second = pl.pallas_call(
        functools.partial(kernel, tiles, regions, scale),
        out_shape=(
            jax.ShapeDtypeStruct((C * NB, BS**3), BF16),
            jax.ShapeDtypeStruct((C * NB, BS**3), BF16),
            jax.ShapeDtypeStruct((27, C, C), F32),
            jax.ShapeDtypeStruct((27, C, C), F32),
        ),
        in_specs=[smem] + [vmem] * 8,
        out_specs=(vmem, vmem, vmem, vmem),
        scratch_shapes=[
            grid,
            grid,
            grid,
            grid,
            grid,
            grid,
            grid,
            grid,
            pltpu.VMEM((2, TOTAL, LANES), F32),
            pltpu.VMEM((2, WIDE_ROWS, 9 * 256), BF16),
            pltpu.VMEM((2, OWN_ROWS, 9 * 256), BF16),
            pltpu.VMEM((2, WIDE_ROWS, 9 * 256), BF16),
            pltpu.VMEM((WIDE_ROWS, 5 * LANES), BF16),
            pltpu.VMEM((4, 9 * 256, 256), BF16),
            pltpu.VMEM((4, 5 * LANES, 256), BF16),
            pltpu.VMEM((GROUPS * LANES, OWN_ROWS), BF16),
            pltpu.VMEM((NPOS + 1, BS * BS, BS * C), F32),
            pltpu.VMEM((2, 2, HALO * Y, 512), BF16),
            pltpu.VMEM((2, 2, HALO * X, 512), BF16),
            pltpu.VMEM((2, 4, 16, 512), BF16),
            pltpu.VMEM((2, 2, HALO * Y, 512), BF16),
            pltpu.VMEM((2, 2, HALO * X, 512), BF16),
            pltpu.VMEM((2, 4, 16, 512), BF16),
            pltpu.VMEM((GROUPS, C * NB, LANES), F32),
            pltpu.VMEM((NB, BS**3, LANES), F32),
            pltpu.VMEM((NB + 1, BS * BS, BS * C), F32),
            pltpu.VMEM((2, SUM_ROWS, LANES), F32),
            pltpu.VMEM((2, tiles, piece, LANES), F32),
            pltpu.VMEM((2, regions, piece, LANES), F32),
            pltpu.VMEM((2, SUM_ROWS, LANES), F32),
            pltpu.SemaphoreType.DMA((2, 8)),
            pltpu.SemaphoreType.DMA((2, 8)),
            pltpu.SemaphoreType.DMA((2, tiles)),
            pltpu.SemaphoreType.DMA((2, tiles)),
            pltpu.SemaphoreType.DMA((2, regions)),
            pltpu.SemaphoreType.DMA((2, regions)),
            pltpu.SemaphoreType.DMA((2, tiles)),
            pltpu.SemaphoreType.DMA((2, tiles)),
        ],
        compiler_params=pltpu.CompilerParams(
            collective_id=0, has_side_effects=True, vmem_limit_bytes=60 * 1024 * 1024
        ),
    )(
        positions,
        flatten(features),
        flatten(cotangent),
        weight_first,
        weight_second,
        row(gain_first),
        row(bias_first),
        row(gain_second),
        row(bias_second),
    )
    shape = (1, C, NB, BS**3)
    return block_output.reshape(shape), block_grad.reshape(shape), grad_first, grad_second


def solution(mesh):
    split = P("rep", None, "tile", None)
    tiles, regions = mesh.shape["tile"], mesh.shape["rep"]
    return jax.shard_map(
        functools.partial(per_device, tiles, regions),
        mesh=mesh,
        in_specs=(split, split, P("rep", "tile"), P(), P(), P(), P(), P(), P()),
        out_specs=(split, split, P(), P()),
        check_vma=False,
    )
```

```python
import functools

import jax
import jax.numpy as jnp
from jax import lax
from jax.experimental import pallas as pl
from jax.experimental.pallas import tpu as pltpu
from jax.sharding import PartitionSpec as P

BS = 8
PX = 4
PY = 2
PZ = 2
TGY = 4
C = 32
X = PX * BS
Y = PY * BS
NPOS = PX * PY * PZ
NB = 8
HALO = 2
YS = Y + 2 * HALO
ROWS = (X + 2 * HALO) * YS
BASE = 16
TOTAL = BASE + ROWS + 16
WIDE_START, WIDE_ROWS = 8, 704
OWN_START, OWN_ROWS = HALO * YS, X * YS
EMPTY = 1024.0
SUM_ROWS = 256
GROUPS = 4
LANES = 128
F32 = jnp.float32
BF16 = jnp.bfloat16
MESH = pl.DeviceIdType.MESH
SHIFTS = [(t // 3 - 1) * YS + (t % 3 - 1) for t in range(9)]
WAYS = [(-1, 0), (1, 0), (0, -1), (0, 1), (-1, -1), (-1, 1), (1, -1), (1, 1)]


def first_cell(way, extent):
    return HALO if way < 0 else extent


def landing_cell(way, extent):
    return HALO + extent if way < 0 else 0


def sigmoid(values):
    return 0.5 + 0.5 * jnp.tanh(0.5 * values)


def kernel(
    tiles,
    regions,
    scale,
    positions,
    feats,
    cots,
    weight_first,
    weight_second,
    gain_first,
    bias_first,
    gain_second,
    bias_second,
    out_ref,
    grad_ref,
    wgrad_first,
    wgrad_second,
    raw,
    field,
    slope_one,
    hidden,
    cot,
    d_two,
    e_two,
    e_one,
    edge,
    taps_one,
    taps_two,
    taps_back,
    corner_taps,
    band,
    band_corner,
    turned,
    staged,
    send_x,
    send_y,
    send_c,
    recv_x,
    recv_y,
    recv_c,
    flat,
    spun,
    blocks,
    sums,
    scattered,
    parts,
    totals,
    send_sem,
    recv_sem,
    scatter_send,
    scatter_recv,
    part_send,
    part_recv,
    total_send,
    total_recv,
):
    me = lax.axis_index("tile")
    rep_me = lax.axis_index("rep")
    tiles_x = tiles // TGY
    piece = SUM_ROWS // tiles
    tx = me // TGY
    ty = me % TGY

    def exists(way, sign):
        ix, iy = tx + sign * way[0], ty + sign * way[1]
        return (ix >= 0) & (ix < tiles_x) & (iy >= 0) & (iy < TGY)

    def partner(way, sign):
        return me + sign * (way[0] * TGY + way[1])

    recv_x[0] = jnp.full(recv_x.shape[1:], EMPTY, BF16)
    recv_y[0] = jnp.full(recv_y.shape[1:], EMPTY, BF16)
    recv_c[0] = jnp.full(recv_c.shape[1:], EMPTY, BF16)
    recv_x[1] = jnp.zeros(recv_x.shape[1:], BF16)
    recv_y[1] = jnp.zeros(recv_y.shape[1:], BF16)
    recv_c[1] = jnp.zeros(recv_c.shape[1:], BF16)

    barrier = pltpu.get_barrier_semaphore()
    for k in range(1, tiles):
        pl.semaphore_signal(
            barrier, inc=1, device_id={"tile": lax.rem(me + k, tiles)}, device_id_type=MESH
        )
    for k in range(1, regions):
        pl.semaphore_signal(
            barrier, inc=1, device_id={"rep": lax.rem(rep_me + k, regions)}, device_id_type=MESH
        )

    def buffers(which, number):
        if number < 2:
            return send_x.at[which, number], recv_x.at[which, number]
        if number < 4:
            return send_y.at[which, number - 2], recv_y.at[which, number - 2]
        return send_c.at[which, number - 4], recv_c.at[which, number - 4]

    def transfer(which, number, sign):
        source, target = buffers(which, number)
        return pltpu.make_async_remote_copy(
            src_ref=source,
            dst_ref=target,
            send_sem=send_sem.at[which, number],
            recv_sem=recv_sem.at[which, number],
            device_id={"tile": partner(WAYS[number], sign)},
            device_id_type=MESH,
        )

    def pack(grid, which):
        for number, (wx, wy) in enumerate(WAYS):
            for g in range(GROUPS):
                lanes = slice(g * LANES, (g + 1) * LANES)
                if number < 2:
                    for k in range(HALO):
                        row = BASE + (first_cell(wx, X) + k) * YS + HALO
                        send_x[which, number, k * Y : (k + 1) * Y, lanes] = grid[
                            g, row : row + Y, :
                        ].astype(BF16)
                elif number < 4:
                    for k in range(HALO):
                        row = BASE + OWN_START + first_cell(wy, Y) + k
                        send_y[which, number - 2, k * X : (k + 1) * X, lanes] = grid[
                            g, pl.ds(row, X, stride=YS), :
                        ].astype(BF16)
                else:
                    row = BASE + first_cell(wx, X) * YS + first_cell(wy, Y)
                    both = [grid[g, row + k * YS : row + k * YS + 8, :] for k in range(HALO)]
                    send_c[which, number - 4, :, lanes] = jnp.concatenate(both, 0).astype(BF16)

    def start(which):
        for number, way in enumerate(WAYS):
            @pl.when(exists(way, 1))
            def _():
                transfer(which, number, 1).start()

    def finish(which):
        for number, way in enumerate(WAYS):
            @pl.when(exists(way, 1))
            def _():
                transfer(which, number, 1).wait_send()

            @pl.when(exists(way, -1))
            def _():
                transfer(which, number, -1).wait_recv()

    def unpack(grid, which):
        for number, (wx, wy) in enumerate(WAYS):
            for g in range(GROUPS):
                lanes = slice(g * LANES, (g + 1) * LANES)
                if number < 2:
                    for k in range(HALO):
                        row = BASE + (landing_cell(wx, X) + k) * YS + HALO
                        grid[g, row : row + Y, :] = recv_x[
                            which, number, k * Y : (k + 1) * Y, lanes
                        ].astype(F32)
                elif number < 4:
                    for k in range(HALO):
                        row = BASE + OWN_START + landing_cell(wy, Y) + k
                        grid[g, pl.ds(row, X, stride=YS), :] = recv_y[
                            which, number - 2, k * X : (k + 1) * X, lanes
                        ].astype(F32)
                else:
                    both = recv_c[which, number - 4, :, lanes].astype(F32)
                    for k in range(HALO):
                        row = BASE + (landing_cell(wx, X) + k) * YS + landing_cell(wy, Y)
                        grid[g, row : row + HALO, :] = both[k * 8 : k * 8 + HALO]

    def block_rows(p, i):
        px, py = p // (PY * PZ), p // PZ % PY
        return BASE + (HALO + px * BS + i) * YS + HALO + py * BS

    lane_group = lax.broadcasted_iota(jnp.int32, (C, LANES), 1) // C
    tall_group = lax.broadcasted_iota(jnp.int32, (BS * BS, LANES), 1) // C
    copies = (
        lax.broadcasted_iota(jnp.int32, (C, LANES), 1) % C
        == lax.broadcasted_iota(jnp.int32, (C, LANES), 0)
    ).astype(F32).astype(BF16)

    def slot_at(p):
        slot = NB
        for s in range(NB):
            slot = jnp.where(positions[0, s] == p, s, slot)
        return slot

    slots = [slot_at(p) for p in range(NPOS)]

    def spread(source, grid, empty):
        for g in range(GROUPS):
            flat[g] = source[:, g * LANES : (g + 1) * LANES].astype(F32)
        for s in range(NB):
            for g in range(GROUPS):
                part = flat[g, pl.ds(s, C, stride=NB), :].astype(BF16)
                spun[s, g * LANES : (g + 1) * LANES, :] = lax.dot_general(
                    part, copies, (((0,), (0,)), ((), ())), preferred_element_type=F32
                )
            for half in range(2):
                total = spun[s, pl.ds(half * 4, BS * BS, stride=BS), :]
                for k in range(1, 4):
                    other = spun[s, pl.ds(half * 4 + k, BS * BS, stride=BS), :]
                    total = jnp.where(tall_group == k, other, total)
                blocks[s, :, half * LANES : (half + 1) * LANES] = total
        blocks[NB] = jnp.full(blocks.shape[1:], empty, F32)
        for p in range(NPOS):
            block = blocks[slots[p]]
            for i in range(BS):
                row = block_rows(p, i)
                for half in range(2):
                    grid[p % PZ * 2 + half, row : row + BS, :] = block[
                        i * BS : (i + 1) * BS, half * LANES : (half + 1) * LANES
                    ]

    def collect(grid, result):
        staged[NPOS] = jnp.zeros(staged.shape[1:], F32)
        for p in range(NPOS):
            for half in range(2):
                for i in range(BS):
                    row = block_rows(p, i)
                    staged[p, i * BS : (i + 1) * BS, half * LANES : (half + 1) * LANES] = grid[
                        p % PZ * 2 + half, row : row + BS, :
                    ]
        for s in range(NB):
            block = staged[positions[0, s]]
            for k in range(BS):
                part = block[:, k // 4 * LANES : (k // 4 + 1) * LANES]
                spun[s, pl.ds(k, BS * BS, stride=BS), :] = jnp.where(
                    tall_group == k % 4, part, 0.0
                )
            for g in range(GROUPS):
                flat[g, pl.ds(s, C, stride=NB), :] = lax.dot_general(
                    copies,
                    spun[s, g * LANES : (g + 1) * LANES, :].astype(BF16),
                    (((1,), (1,)), ((), ())),
                    preferred_element_type=F32,
                )
        for g in range(GROUPS):
            result[:, g * LANES : (g + 1) * LANES] = flat[g].astype(BF16)

    def scatter_copy(w, k):
        peer = lax.rem(me + k, tiles)
        return pltpu.make_async_remote_copy(
            src_ref=sums.at[w, pl.ds(pl.multiple_of(peer * piece, 8), piece), :],
            dst_ref=scattered.at[w, k],
            send_sem=scatter_send.at[w, k],
            recv_sem=scatter_recv.at[w, k],
            device_id={"tile": peer},
            device_id_type=MESH,
        )

    def part_copy(w, k):
        return pltpu.make_async_remote_copy(
            src_ref=parts.at[w, rep_me],
            dst_ref=parts.at[w, rep_me],
            send_sem=part_send.at[w, k],
            recv_sem=part_recv.at[w, k],
            device_id={"rep": lax.rem(rep_me + k, regions)},
            device_id_type=MESH,
        )

    own_piece = pl.ds(pl.multiple_of(me * piece, 8), piece)

    def total_copy(w, k):
        return pltpu.make_async_remote_copy(
            src_ref=totals.at[w, own_piece, :],
            dst_ref=totals.at[w, own_piece, :],
            send_sem=total_send.at[w, k],
            recv_sem=total_recv.at[w, k],
            device_id={"tile": lax.rem(me + k, tiles)},
            device_id_type=MESH,
        )

    def scatter_start(w):
        for k in range(1, tiles):
            scatter_copy(w, k).start()

    def scatter_finish(w):
        total = sums[w, own_piece, :]
        for k in range(1, tiles):
            scatter_copy(w, k).wait()
            total = total + scattered[w, k]
        parts[w, rep_me] = total * scale
        for k in range(1, regions):
            part_copy(w, k).start()

    def part_finish(w):
        for k in range(1, regions):
            part_copy(w, k).wait()
        total = parts[w, 0]
        for r in range(1, regions):
            total = total + parts[w, r]
        totals[w, own_piece, :] = total
        for k in range(1, tiles):
            total_copy(w, k).start()

    def total_finish(w, result):
        for k in range(1, tiles):
            total_copy(w, k).wait()
        for q in range(27):
            block = totals[w, q // 4 * C : (q // 4 + 1) * C, :]
            if q % 4:
                block = pltpu.roll(block, LANES - q % 4 * C, 1)
            result[q] = block[:, :C]

    for g in range(GROUPS):
        raw[g] = jnp.full((TOTAL, LANES), EMPTY, F32)
        cot[g] = jnp.zeros((TOTAL, LANES), F32)
        e_two[g] = jnp.zeros((TOTAL, LANES), F32)
    spread(feats, raw, EMPTY)
    pack(raw, 0)
    pl.semaphore_wait(barrier, tiles + regions - 2)
    start(0)

    picks = [(lane_group == k).astype(F32).astype(BF16) for k in range(4)]
    for w in range(4):
        band_corner[w] = jnp.zeros(band_corner.shape[1:], BF16)

    def turned_weight(ref, q):
        block = lax.dot_general(
            ref[q], copies, (((0,), (0,)), ((), ())), preferred_element_type=F32
        )
        return block.astype(BF16)

    def plain_weight(ref, q):
        return jnp.dot(ref[26 - q], copies, preferred_element_type=F32).astype(BF16)

    def build_one(w, ref, read, t):
        three = [read(ref, t * 3 + k) for k in range(3)]
        row = pl.multiple_of(t * 256, 256)
        for z_in in range(8):
            for tile in range(2):
                total = None
                for k in range(4):
                    dz = z_in - (tile * 4 + k)
                    if abs(dz) <= 1:
                        term = three[dz + 1] * picks[k]
                        total = term if total is None else total + term
                if total is None:
                    total = jnp.zeros((C, LANES), BF16)
                band[w, pl.ds(row + z_in * C, C), tile * LANES : (tile + 1) * LANES] = total
        edge_row = pl.multiple_of(t * 64, 64)
        band_corner[w, pl.ds(edge_row, C), LANES:] = three[0] * picks[0]
        band_corner[w, pl.ds(edge_row + C, C), :LANES] = three[2] * picks[3]

    def build(t, carry):
        build_one(0, weight_first, turned_weight, t)
        build_one(1, weight_second, turned_weight, t)
        build_one(2, weight_second, plain_weight, t)
        build_one(3, weight_first, plain_weight, t)
        return carry

    lax.fori_loop(0, 9, build, 0)
    spread(cots, cot, 0.0)

    def gather_taps(grid, taps, first, rows):
        lane = lax.broadcasted_iota(jnp.int32, (TOTAL, LANES), 1)
        pair = jnp.where(
            lane < C,
            pltpu.roll(grid[1], C, 1),
            jnp.where(lane < 2 * C, pltpu.roll(grid[2], C, 1), 0.0),
        )
        edge[0] = pair
        edge[1] = pltpu.roll(pair, 2 * C, 1)
        for t in range(9):
            begin = BASE + first + SHIFTS[t]
            for g in range(GROUPS):
                lanes = slice(t * 256 + g % 2 * LANES, t * 256 + g % 2 * LANES + LANES)
                taps[g // 2, :rows, lanes] = grid[g, begin : begin + rows, :].astype(BF16)
        for j in range(5):
            begin = BASE + first + SHIFTS[2 * j]
            value = edge[0, begin : begin + rows, :]
            if j < 4:
                begin = BASE + first + SHIFTS[2 * j + 1]
                value = value + edge[1, begin : begin + rows, :]
            corner_taps[:rows, j * LANES : (j + 1) * LANES] = value.astype(BF16)

    def convolve(taps, w, first, rows, finish_group):
        chunk = rows // 2

        def step(c, carry):
            here = pl.ds(pl.multiple_of(c * chunk, 16), chunk)
            low = jnp.dot(taps[0, here, :], band[w], preferred_element_type=F32)
            high = jnp.dot(taps[1, here, :], band[w], preferred_element_type=F32)
            mid = jnp.dot(corner_taps[here, :], band_corner[w], preferred_element_type=F32)
            there = pl.ds(pl.multiple_of(BASE + first + c * chunk, 8), chunk)
            finish_group(0, there, low[:, :LANES])
            finish_group(1, there, low[:, LANES:] + mid[:, :LANES])
            finish_group(2, there, high[:, :LANES] + mid[:, LANES:])
            finish_group(3, there, high[:, LANES:])
            return carry

        lax.fori_loop(0, 2, step, 0, unroll=True)

    def weight_gradient(taps, offset, which):
        def step(x_tap, carry):
            lanes = pl.ds(pl.multiple_of(x_tap * 768, 256), 768)
            products = [
                jnp.dot(
                    turned[half * 224 : half * 224 + 288, :],
                    taps[half, offset : offset + OWN_ROWS, lanes],
                    preferred_element_type=F32,
                )
                for half in range(2)
            ]
            for y_tap in range(3):
                for dz in range(-1, 2):
                    total = jnp.zeros((C, LANES), F32)
                    for half in range(2):
                        for b in range(8):
                            a = b + half - dz
                            if 0 <= a <= 8:
                                begin = y_tap * 256 + b // 4 * LANES
                                part = products[half][a * C : (a + 1) * C, begin : begin + LANES]
                                total = total + jnp.where(lane_group == b % 4, part, 0.0)
                    total = total + pltpu.roll(total, 64, 1)
                    total = total + pltpu.roll(total, 32, 1)
                    q = x_tap * 9 + (y_tap * 3 + dz + 1)
                    rows = pl.ds(pl.multiple_of(lax.div(q, 4) * C, C), C)
                    sums[which, rows, :] += jnp.where(lane_group == lax.rem(q, 4), total, 0.0)
            return carry

        lax.fori_loop(0, 3, step, 0, unroll=True)

    def wide(ref):
        return jnp.concatenate([ref[...]] * 4, axis=1)

    sums[...] = jnp.zeros(sums.shape, F32)
    gain_one, bias_one = wide(gain_first), wide(bias_first)
    gain_two, bias_two = wide(gain_second), wide(bias_second)

    finish(0)
    unpack(raw, 0)
    for g in range(GROUPS):
        value = raw[g]
        field[g] = jnp.where(value < 512.0, value, 0.0)

    gather_taps(field, taps_one, WIDE_START, WIDE_ROWS)

    def after_first(g, rows, value):
        pre = value * gain_one + bias_one
        active = raw[g, rows, :] < 512.0
        s = sigmoid(pre)
        act = pre * s
        slope = (s + act * (1.0 - s)) * gain_one
        slope_one[g, rows, :] = jnp.where(active, slope, 0.0)
        hidden[g, rows, :] = jnp.where(active, act, 0.0).astype(BF16).astype(F32)

    convolve(taps_one, 0, WIDE_START, WIDE_ROWS, after_first)

    gather_taps(hidden, taps_two, OWN_START, OWN_ROWS)

    def after_second(g, rows, value):
        pre = value * gain_two + bias_two + field[g, rows, :]
        s = sigmoid(pre)
        act = pre * s
        hidden[g, rows, :] = act
        d = cot[g, rows, :] * (s + act * (1.0 - s))
        d_two[g, rows, :] = d
        e_two[g, rows, :] = (d * gain_two).astype(BF16).astype(F32)

    convolve(taps_two, 1, OWN_START, OWN_ROWS, after_second)

    pack(e_two, 1)
    start(1)
    own = slice(BASE + OWN_START, BASE + OWN_START + OWN_ROWS)
    for g in range(GROUPS):
        turned[g * LANES : (g + 1) * LANES, :] = jnp.transpose(e_two[g, own, :]).astype(BF16)
    weight_gradient(taps_two, 0, 1)
    scatter_start(1)
    collect(hidden, out_ref)
    finish(1)
    unpack(e_two, 1)

    gather_taps(e_two, taps_back, WIDE_START, WIDE_ROWS)

    def after_third(g, rows, value):
        e_one[g, rows, :] = (value * slope_one[g, rows, :]).astype(BF16).astype(F32)

    convolve(taps_back, 2, WIDE_START, WIDE_ROWS, after_third)

    scatter_finish(1)
    y_cell = lax.rem(lax.broadcasted_iota(jnp.int32, (OWN_ROWS, LANES), 0), YS)
    inside = (y_cell >= HALO) & (y_cell < HALO + Y)
    for g in range(GROUPS):
        turned[g * LANES : (g + 1) * LANES, :] = jnp.transpose(
            jnp.where(inside, e_one[g, own, :], 0.0)
        ).astype(BF16)
    weight_gradient(taps_one, OWN_START - WIDE_START, 0)
    scatter_start(0)
    part_finish(1)

    gather_taps(e_one, taps_back, OWN_START, OWN_ROWS)
    scatter_finish(0)

    def after_fourth(g, rows, value):
        d_two[g, rows, :] = d_two[g, rows, :] + value

    convolve(taps_back, 3, OWN_START, OWN_ROWS, after_fourth)
    part_finish(0)
    collect(d_two, grad_ref)
    total_finish(1, wgrad_second)
    total_finish(0, wgrad_first)


def per_device(
    tiles,
    regions,
    features,
    cotangent,
    positions,
    weight_first,
    weight_second,
    gain_first,
    bias_first,
    gain_second,
    bias_second,
):
    def flatten(array):
        return array.reshape(C * NB, BS**3)

    def row(vector):
        return vector.reshape(1, C)

    scale = 1.0 / float(tiles * regions * NB * BS**3) ** 0.5
    piece = SUM_ROWS // tiles
    grid = pltpu.VMEM((GROUPS, TOTAL, LANES), F32)
    smem = pl.BlockSpec(memory_space=pltpu.SMEM)
    vmem = pl.BlockSpec(memory_space=pltpu.VMEM)
    block_output, block_grad, grad_first, grad_second = pl.pallas_call(
        functools.partial(kernel, tiles, regions, scale),
        out_shape=(
            jax.ShapeDtypeStruct((C * NB, BS**3), BF16),
            jax.ShapeDtypeStruct((C * NB, BS**3), BF16),
            jax.ShapeDtypeStruct((27, C, C), F32),
            jax.ShapeDtypeStruct((27, C, C), F32),
        ),
        in_specs=[smem] + [vmem] * 8,
        out_specs=(vmem, vmem, vmem, vmem),
        scratch_shapes=[
            grid,
            grid,
            grid,
            grid,
            grid,
            grid,
            grid,
            grid,
            pltpu.VMEM((2, TOTAL, LANES), F32),
            pltpu.VMEM((2, WIDE_ROWS, 9 * 256), BF16),
            pltpu.VMEM((2, OWN_ROWS, 9 * 256), BF16),
            pltpu.VMEM((2, WIDE_ROWS, 9 * 256), BF16),
            pltpu.VMEM((WIDE_ROWS, 5 * LANES), BF16),
            pltpu.VMEM((4, 9 * 256, 256), BF16),
            pltpu.VMEM((4, 5 * LANES, 256), BF16),
            pltpu.VMEM((GROUPS * LANES, OWN_ROWS), BF16),
            pltpu.VMEM((NPOS + 1, BS * BS, BS * C), F32),
            pltpu.VMEM((2, 2, HALO * Y, 512), BF16),
            pltpu.VMEM((2, 2, HALO * X, 512), BF16),
            pltpu.VMEM((2, 4, 16, 512), BF16),
            pltpu.VMEM((2, 2, HALO * Y, 512), BF16),
            pltpu.VMEM((2, 2, HALO * X, 512), BF16),
            pltpu.VMEM((2, 4, 16, 512), BF16),
            pltpu.VMEM((GROUPS, C * NB, LANES), F32),
            pltpu.VMEM((NB, BS**3, LANES), F32),
            pltpu.VMEM((NB + 1, BS * BS, BS * C), F32),
            pltpu.VMEM((2, SUM_ROWS, LANES), F32),
            pltpu.VMEM((2, tiles, piece, LANES), F32),
            pltpu.VMEM((2, regions, piece, LANES), F32),
            pltpu.VMEM((2, SUM_ROWS, LANES), F32),
            pltpu.SemaphoreType.DMA((2, 8)),
            pltpu.SemaphoreType.DMA((2, 8)),
            pltpu.SemaphoreType.DMA((2, tiles)),
            pltpu.SemaphoreType.DMA((2, tiles)),
            pltpu.SemaphoreType.DMA((2, regions)),
            pltpu.SemaphoreType.DMA((2, regions)),
            pltpu.SemaphoreType.DMA((2, tiles)),
            pltpu.SemaphoreType.DMA((2, tiles)),
        ],
        compiler_params=pltpu.CompilerParams(
            collective_id=0, has_side_effects=True, vmem_limit_bytes=60 * 1024 * 1024
        ),
    )(
        positions,
        flatten(features),
        flatten(cotangent),
        weight_first,
        weight_second,
        row(gain_first),
        row(bias_first),
        row(gain_second),
        row(bias_second),
    )
    shape = (1, C, NB, BS**3)
    return block_output.reshape(shape), block_grad.reshape(shape), grad_first, grad_second


def solution(mesh):
    split = P("rep", None, "tile", None)
    tiles, regions = mesh.shape["tile"], mesh.shape["rep"]
    return jax.shard_map(
        functools.partial(per_device, tiles, regions),
        mesh=mesh,
        in_specs=(split, split, P("rep", "tile"), P(), P(), P(), P(), P(), P()),
        out_specs=(split, split, P(), P()),
        check_vma=False,
    )
```
